32 devices in a mesh: dp: 2 (over x), space: 16 (over z, y, core).
Axes of the slice: x: 2, y: 2, z: 4, core: 2. Of those that a mesh axis runs over, the one named last changes fastest.
Arguments:
- inputs: float32 [2, 32, 128, 128, 128], P('dp', None, 'space'), may hold values from -6 to 6
- preact: float32 [2, 32, 128, 128, 128], P('dp', None, 'space'), may hold values from -6 to 6
- cotangent: float32 [2, 32, 128, 128, 128], P('dp', None, 'space'), may hold values from -6 to 6
- spectral_weight: float32 [32, 1024, 2048], P(None, 'space'), may hold values from -3 to 3
- skip_weight: float32 [32, 32], replicated, may hold values from -1 to 1
Outputs:
- input_grad: float32 [2, 32, 128, 128, 128], P('dp', None, 'space')
- weight_grad: float32 [32, 1024, 2048], P('dp', 'space')
- skip_grad: float32 [32, 32], replicated
The draws below stay inside these ranges and needn't reach their ends.
All inputs are finite; a program needn't handle non-finite values.
Results may differ from the reference program's by a relative error of at most 0.00016.
Values sent between devices are 32-bit elements; how exact they have to be, the bound alone decides.
A program may use at most 256 MiB of HBM per device.

```python
import jax
import jax.numpy as jnp
from jax import lax

N = 128
C = 32
MX = 32
MY = 64
MZ = 16
BATCH = 2


def block_scale(stream_key, extent, cuts, low, high):
    def one(dim, parts):
        steps = jax.random.uniform(jax.random.fold_in(jax.random.fold_in(stream_key, 6), dim), (parts,), jnp.float32, low / len(cuts), high / len(cuts))
        return jnp.repeat(jnp.exp(steps), extent[dim] // parts).reshape((-1,) + (1,) * (len(extent) - dim - 1))

    loudness = one(*cuts[0])
    for cut in cuts[1:]:
        loudness = loudness * one(*cut)
    return loudness


def gaussian(key, dims, scale, reach, split=(), held_as=jnp.bfloat16):
    entries = jax.random.normal(key, dims, jnp.float32) * scale
    if len(split) > 0:
        entries = block_scale(key, dims, split, -0.22, 0.18) * entries
    return jnp.clip(entries, min=-reach, max=reach).astype(held_as)


def setup_inputs(seed: int = 0) -> dict:
    arg_keys = jax.random.split(jax.random.key(seed), 6)
    inputs = gaussian(arg_keys[0], (BATCH, C, N, N, N), 1.0, 6.0, ((0, 2), (2, 16)), jnp.float32)
    preact = gaussian(arg_keys[1], (BATCH, C, N, N, N), 1.5, 6.0, ((0, 2), (2, 16)), jnp.float32)
    cotangent = gaussian(arg_keys[2], (BATCH, C, N, N, N), 1.0, 6.0, ((0, 2), (2, 16)), jnp.float32)
    spectral_weight = gaussian(arg_keys[3], (MX, MY * MZ, 2 * C * C), 0.5, 3.0, ((1, 16),), jnp.float32)
    skip_weight = gaussian(arg_keys[4], (C, C), C ** -0.5, 1.0, (), jnp.float32)
    return {"inputs": inputs, "preact": preact, "cotangent": cotangent, "spectral_weight": spectral_weight, "skip_weight": skip_weight}


highest = lax.Precision.HIGHEST
tanh_scale = 0.7978845608028654
cubic_term = 0.044715


def gelu_slope(preact):
    bounded = jnp.tanh(tanh_scale * (preact + cubic_term * preact * preact * preact))
    return 0.5 * (1.0 + bounded) + 0.5 * preact * (1.0 - bounded * bounded) * tanh_scale * (1.0 + 3.0 * cubic_term * preact * preact)


def signed_modes(modes_count):
    positions = jnp.arange(modes_count, dtype=jnp.int32)
    return jnp.where(positions < modes_count // 2, positions, positions - modes_count)


def phases(frequency, grid_size):
    points = jnp.arange(grid_size, dtype=jnp.int32)
    product = jnp.mod(frequency[:, None] * points[None, :], grid_size)
    return (2.0 * jnp.pi / grid_size) * product.astype(jnp.float32)


def make_tables(grid_size, modes_x, modes_y, modes_z):
    angle_y = phases(signed_modes(modes_y), grid_size)
    angle_z = phases(jnp.arange(modes_z, dtype=jnp.int32), grid_size)
    angle_x = phases(signed_modes(modes_x), grid_size)
    cos_y, sin_y = jnp.cos(angle_y), jnp.sin(angle_y)
    cos_z, sin_z = jnp.cos(angle_z), jnp.sin(angle_z)
    cos_x, sin_x = jnp.cos(angle_x), jnp.sin(angle_x)
    forward_y = jnp.stack([cos_y.T, -sin_y.T], 1)
    forward_z = jnp.stack([jnp.stack([cos_z.T, -sin_z.T], 1), jnp.stack([sin_z.T, cos_z.T], 1)], 0)
    forward_x = jnp.stack([jnp.stack([cos_x.T, -sin_x.T], 1), jnp.stack([sin_x.T, cos_x.T], 1)], 0)
    inverse_x = jnp.stack([jnp.stack([cos_x, sin_x], 1), jnp.stack([-sin_x, cos_x], 1)], 0)
    inverse_z = jnp.stack([jnp.stack([cos_z, sin_z], 1), jnp.stack([-sin_z, cos_z], 1)], 0)
    inverse_y = jnp.stack([cos_y, -sin_y], 1)
    return forward_y, forward_z, forward_x, inverse_x, inverse_z, inverse_y


def transform_yz(field, forward_y, forward_z):
    halfway = jnp.einsum("bcxyz,yrj->bcxrjz", field, forward_y, precision=highest)
    mixed = jnp.einsum("bcxrjz,rzsn->sbcxnj", halfway, forward_z, precision=highest)
    return mixed.reshape(mixed.shape[:4] + (mixed.shape[4] * mixed.shape[5],))


def transform_x(stacked, forward_x, norm_scale):
    return jnp.einsum("rbcxk,rxsm->sbcmk", stacked, forward_x, precision=highest) * norm_scale


def weight_terms(spectra, input_spectra):
    real_part = jnp.einsum("bomk,bimk->mkoi", spectra[0], input_spectra[0], precision=highest)
    real_part = real_part + jnp.einsum("bomk,bimk->mkoi", spectra[1], input_spectra[1], precision=highest)
    imag_part = jnp.einsum("bomk,bimk->mkoi", spectra[1], input_spectra[0], precision=highest)
    imag_part = imag_part - jnp.einsum("bomk,bimk->mkoi", spectra[0], input_spectra[1], precision=highest)
    stacked = jnp.stack([real_part, imag_part], 2)
    return stacked.reshape(stacked.shape[0], stacked.shape[1], -1)


def mode_products(weights, spectra):
    channels = spectra.shape[2]
    pieces = weights.reshape(weights.shape[0], weights.shape[1], 2, channels, channels)
    weight_real = pieces[:, :, 0]
    weight_imag = pieces[:, :, 1]
    real_part = jnp.einsum("mkoi,bomk->bimk", weight_real, spectra[0], precision=highest)
    real_part = real_part + jnp.einsum("mkoi,bomk->bimk", weight_imag, spectra[1], precision=highest)
    imag_part = jnp.einsum("mkoi,bomk->bimk", weight_real, spectra[1], precision=highest)
    imag_part = imag_part - jnp.einsum("mkoi,bomk->bimk", weight_imag, spectra[0], precision=highest)
    return jnp.stack([real_part, imag_part], 0)


def restore_x(dual, inverse_x):
    return jnp.einsum("rbcmk,rmsx->sbcxk", dual, inverse_x, precision=highest)


def restore_yz(stacked, inverse_z, inverse_y):
    depth_modes = inverse_z.shape[1]
    shaped = stacked.reshape(stacked.shape[:4] + (depth_modes, stacked.shape[4] // depth_modes))
    planes = jnp.einsum("rbcxnj,rnsz->bcxjsz", shaped, inverse_z, precision=highest)
    return jnp.einsum("bcxjsz,jsy->bcxyz", planes, inverse_y, precision=highest)


def reference(inputs, preact, cotangent, spectral_weight, skip_weight):
    norm_scale = float(N) ** -1.5
    tables = make_tables(N, MX, MY, MZ)
    grad_pre = cotangent * gelu_slope(preact)

    def per_sample(field):
        return transform_x(transform_yz(field[None], tables[0], tables[1]), tables[2], norm_scale)[:, 0]

    spec_grad = jnp.moveaxis(lax.map(per_sample, grad_pre), 0, 1)
    spec_input = jnp.moveaxis(lax.map(per_sample, inputs), 0, 1)
    weight_grad = weight_terms(spec_grad, spec_input)
    dual = mode_products(spectral_weight, spec_grad)

    def back_sample(piece):
        return restore_yz(restore_x(piece[:, None], tables[3]), tables[4], tables[5])[0]

    spatial = lax.map(back_sample, jnp.moveaxis(dual, 1, 0))
    skip_term = jnp.einsum("oi,boxyz->bixyz", skip_weight, grad_pre, precision=highest)
    input_grad = norm_scale * spatial + skip_term
    skip_grad = norm_scale * jnp.einsum("boxyz,bixyz->oi", grad_pre, inputs, precision=highest)
    return input_grad, weight_grad, skip_grad
```

```python
import functools

import jax
import jax.numpy as jnp
import ml_dtypes
import numpy as np
from jax import lax
from jax.experimental import pallas as pl
from jax.experimental.pallas import tpu as pltpu
from jax.sharding import PartitionSpec as P

N = 128
C = 32
MX = 32
MY = 64
MZ = 16
NORM = float(N) ** -1.5

tanh_scale = 0.7978845608028654
cubic_term = 0.044715
BF = jnp.bfloat16
F32 = jnp.float32
LIMIT = 48 * 1024 * 1024


def signed(count):
    p = np.arange(count)
    return np.where(p < count // 2, p, p - count)


def waves(freq):
    angle = 2 * np.pi / N * np.mod(freq[:, None] * np.arange(N)[None, :], N)
    return np.cos(angle), np.sin(angle)


def halves(table):
    hi = table.astype(np.float32).astype(ml_dtypes.bfloat16)
    lo = (table - hi.astype(np.float64)).astype(np.float32).astype(ml_dtypes.bfloat16)
    return hi, lo


def make_tables():
    cx, sx = waves(signed(MX))
    cy, sy = waves(signed(MY))
    cz, sz = waves(np.arange(MZ))
    t = {}
    t["zf"] = np.concatenate(halves(np.concatenate([cz, -sz], 0)), 0)
    hi, lo = halves(np.block([[cy.T, -sy.T], [sy.T, cy.T]]))
    t["yf"] = np.concatenate([hi, hi, lo], 0)
    hi, lo = halves(np.concatenate([cx, sx], 0))
    t["xf"] = np.concatenate([hi, lo, hi], 1)
    t["xi"] = np.concatenate([hi.T, lo.T, hi.T], 1)
    hi, lo = halves(np.block([[cy, sy], [-sy, cy]]))
    t["yi"] = np.concatenate([hi, hi, lo], 0)
    hi, lo = halves(np.concatenate([cz, -sz], 0))
    t["zi"] = np.concatenate([hi, hi, lo], 0)
    eye = np.eye(C)
    spread_out = np.repeat(eye, C, axis=1)
    spread_in = np.tile(eye, (1, C))
    t["eo"] = np.concatenate([spread_out, spread_out], 0).astype(ml_dtypes.bfloat16)
    t["ei"] = np.concatenate([spread_in, spread_in], 0).astype(ml_dtypes.bfloat16)
    return t


def split(x):
    hi = x.astype(BF)
    lo = (x - hi.astype(F32)).astype(BF)
    return hi, lo


def nn(a, b):
    return lax.dot_general(a, b, (((1,), (0,)), ((), ())), preferred_element_type=F32)


def nt(a, b):
    return lax.dot_general(a, b, (((1,), (1,)), ((), ())), preferred_element_type=F32)


def tn(a, b):
    return lax.dot_general(a, b, (((0,), (0,)), ((), ())), preferred_element_type=F32)


def gelu_slope(h):
    t = jnp.tanh(tanh_scale * (h + cubic_term * h * h * h))
    return 0.5 * (1.0 + t) + 0.5 * h * (1.0 - t * t) * tanh_scale * (1.0 + 3.0 * cubic_term * h * h)


GROUP = 8


def planes_forward(d, first, zf_ref, yf_ref, out2d):
    hi, lo = split(d.reshape(GROUP * N, N))
    a = nt(zf_ref[...], hi)
    z = a[: 2 * MZ] + a[2 * MZ :] + nt(zf_ref[: 2 * MZ, :], lo)
    rows = []
    for c in range(GROUP):
        cols = slice(c * N, (c + 1) * N)
        rows.append(jnp.concatenate([z[:MZ, cols], z[MZ:, cols]], 1))
    hi, lo = split(jnp.concatenate(rows, 0))
    y = nn(jnp.concatenate([hi, lo, hi], 1), yf_ref[...])
    for c in range(GROUP):
        out2d[pl.ds(first + c, MZ, stride=C), :] = y[c * MZ : (c + 1) * MZ, :]


def grad_kernel(pre_ref, cot_ref, zf_ref, yf_ref, gp_ref, out_ref):
    out2d = out_ref.reshape(MZ * C, 2 * MY)
    for g in range(0, C, GROUP):
        gp = cot_ref[0, g : g + GROUP, 0] * gelu_slope(pre_ref[0, g : g + GROUP, 0])
        gp_ref[0, g : g + GROUP, 0] = gp
        planes_forward(gp, g, zf_ref, yf_ref, out2d)


def input_kernel(in_ref, gp_ref, zf_ref, yf_ref, out_ref, acc_ref):
    out2d = out_ref.reshape(MZ * C, 2 * MY)

    @pl.when(pl.program_id(0) == 0)
    def _():
        acc_ref[...] = jnp.zeros_like(acc_ref)

    for g in range(0, C, GROUP):
        planes_forward(in_ref[0, g : g + GROUP, 0], g, zf_ref, yf_ref, out2d)

    def rows(ref, y):
        a = ref[0, :, 0, pl.ds(y, 8), :].reshape(C * 8, N)
        b = ref[0, :, 0, pl.ds(y + 8, 8), :].reshape(C * 8, N)
        return split(jnp.concatenate([a, b], 1))

    @pl.loop(0, N // 16)
    def _(s):
        y = pl.multiple_of(s * 16, 16)
        gh, gl = rows(gp_ref, y)
        ih, il = rows(in_ref, y)
        acc_ref[...] += nt(
            jnp.concatenate([gh, gl, gh], 1), jnp.concatenate([ih, ih, il], 1)
        )


def swap(x):
    return pltpu.roll(x, MY, 1)


def lane_sign(rows, first):
    lane = lax.broadcasted_iota(jnp.int32, (rows, 2 * MY), 1)
    return jnp.where(lane < MY, first, -first).astype(F32)


def x_forward(a2d, xf_ref):
    for c in range(C):
        hi, lo = split(a2d[pl.ds(c, N, stride=C), :])
        p = nn(xf_ref[...], jnp.concatenate([hi, hi, lo], 0))
        s = (p[:MX] + lane_sign(MX, 1.0) * swap(p[MX:])) * NORM
        yield c, s


def modes_kernel(a_ref, w_ref, xf_ref, xi_ref, eo_ref, s_ref, out_ref, d_ref, *, dp, step):
    mh = MX // dp
    a2d = a_ref.reshape(N * C, 2 * MY)
    s2d = s_ref.reshape(MX * C, 2 * MY)
    out2d = out_ref.reshape(N * C, 2 * MY)
    pid = pl.program_id(0)

    @pl.when(pid == 0)
    def _():
        for c, s in x_forward(a2d, xf_ref):
            for h in range(dp):
                s_ref[h, c] = s[h * mh : (h + 1) * mh]

    for u in range(step):
        m = pid * step + u
        start = (m // mh) * (C * mh) + m % mh
        hi, lo = split(s2d[pl.ds(start, C, stride=mh), :])
        g = tn(jnp.concatenate([hi, lo], 0), eo_ref[...])
        gr, gi = g[:MY], g[MY:]
        wr, wi = w_ref[u, :, : C * C], w_ref[u, :, C * C :]

        def fold(x):
            total = x[:, :128]
            for t in range(1, C * C // 128):
                total = total + x[:, t * 128 : (t + 1) * 128]
            return total

        both = jnp.concatenate([fold(wr * gr + wi * gi), fold(wr * gi - wi * gr)], 0).T
        total = both[:C] + both[C : 2 * C] + both[2 * C : 3 * C] + both[3 * C :]
        d_ref[pl.ds(m, C, stride=MX), :] = total * NORM

    @pl.when(pid == MX // step - 1)
    def _():
        for i in range(C):
            d = d_ref[i * MX : (i + 1) * MX, :]
            hi, lo = split(jnp.concatenate([d, lane_sign(MX, -1.0) * swap(d)], 0))
            out2d[pl.ds(i, N, stride=C), :] = nn(xi_ref[...], jnp.concatenate([hi, hi, lo], 0))


def spectrum_kernel(a_ref, xf_ref, s_ref, *, dp):
    mh = MX // dp
    a2d = a_ref.reshape(N * C, 2 * MY)
    for c, s in x_forward(a2d, xf_ref):
        for h in range(dp):
            s_ref[h, c] = s[h * mh : (h + 1) * mh]


def weight_kernel(g_ref, i_ref, eo_ref, ei_ref, out_ref, *, dp, step):
    mh = MX // dp
    g2d = g_ref.reshape(MX * C, 2 * MY)
    i2d = i_ref.reshape(MX * C, 2 * MY)
    for u in range(step):
        m = pl.program_id(0) * step + u
        real = imag = None
        for b in range(dp):
            at = pl.ds(b * (C * mh) + m, C, stride=mh)
            g = tn(jnp.concatenate(split(g2d[at, :]), 0), eo_ref[...])
            i = tn(jnp.concatenate(split(i2d[at, :]), 0), ei_ref[...])
            gr, gi, ir, ii = g[:MY], g[MY:], i[:MY], i[MY:]
            r = gr * ir + gi * ii
            j = gi * ir - gr * ii
            real, imag = (r, j) if real is None else (real + r, imag + j)
        out_ref[u, :, : C * C] = real
        out_ref[u, :, C * C :] = imag


def inverse_kernel(b_ref, gp_ref, k_ref, yi_ref, zi_ref, out_ref, re_ref, im_ref):
    hi, lo = split(b_ref.reshape(MZ * C, 2 * MY)[...])
    v = nn(jnp.concatenate([hi, lo, hi], 1), yi_ref[...])
    re_ref[...] = v[:, :N]
    im_ref[...] = v[:, N:]
    for i in range(C):
        at = pl.ds(i, MZ, stride=C)
        hi, lo = split(jnp.concatenate([re_ref[at, :], im_ref[at, :]], 0))
        out_ref[0, i, 0] = tn(jnp.concatenate([hi, lo, hi], 0), zi_ref[...])
    kh, kl = split(k_ref[...])
    k3 = jnp.concatenate([kh, kl, kh], 1)

    @pl.loop(0, N // 16)
    def _(s):
        y = pl.multiple_of(s * 16, 16)
        a = gp_ref[0, :, 0, pl.ds(y, 8), :].reshape(C * 8, N)
        b = gp_ref[0, :, 0, pl.ds(y + 8, 8), :].reshape(C * 8, N)
        gh, gl = split(jnp.concatenate([a, b], 1))
        r = nn(k3, jnp.concatenate([gh, gh, gl], 0))
        out_ref[0, :, 0, pl.ds(y, 8), :] += r[:, :N].reshape(C, 8, N)
        out_ref[0, :, 0, pl.ds(y + 8, 8), :] += r[:, N:].reshape(C, 8, N)


def whole(shape):
    return pl.BlockSpec(shape, lambda *_: (0,) * len(shape))


def params():
    return pltpu.CompilerParams(vmem_limit_bytes=LIMIT)


def cost(flops, nbytes):
    return pl.CostEstimate(flops=int(flops), bytes_accessed=int(nbytes), transcendentals=0)


def body(space, dp, inputs, preact, cotangent, spectral_weight, skip_weight):
    t = {k: jnp.asarray(v) for k, v in make_tables().items()}
    xl = inputs.shape[2]
    kl = spectral_weight.shape[1]
    field = jax.ShapeDtypeStruct(inputs.shape, F32)
    spread = jax.ShapeDtypeStruct((MZ, xl, C, 2 * MY), F32)
    plane = pl.BlockSpec((1, C, 1, N, N), lambda x: (0, 0, x, 0, 0))
    lines = pl.BlockSpec((MZ, 1, C, 2 * MY), lambda x: (0, x, 0, 0))
    nbytes = inputs.size * 4

    gp, part_g = pl.pallas_call(
        grad_kernel,
        grid=(xl,),
        in_specs=[plane, plane, whole(t["zf"].shape), whole(t["yf"].shape)],
        out_specs=[plane, lines],
        out_shape=[field, spread],
        compiler_params=params(),
        cost_estimate=cost(nbytes * 300, nbytes * 4),
        name="grad_forward",
    )(preact, cotangent, t["zf"], t["yf"])
    part_i, acc = pl.pallas_call(
        input_kernel,
        grid=(xl,),
        in_specs=[plane, plane, whole(t["zf"].shape), whole(t["yf"].shape)],
        out_specs=[lines, whole((C * 8, C * 8))],
        out_shape=[spread, jax.ShapeDtypeStruct((C * 8, C * 8), F32)],
        compiler_params=params(),
        cost_estimate=cost(nbytes * 600, nbytes * 3),
        name="input_forward",
    )(inputs, gp, t["zf"], t["yf"])
    diag = jnp.einsum("oyiy->oi", acc.reshape(C, 8, C, 8), precision=lax.Precision.HIGHEST)
    skip_grad = lax.psum(NORM * diag, ("dp", "space"))

    q = space // MZ
    jl = MY // q

    def outward(part):
        p = part.reshape(MZ, xl, C, 2, q, jl).transpose(0, 4, 1, 2, 3, 5)
        p = p.reshape(space, xl, C, 2 * jl)
        return lax.all_to_all(p, "space", split_axis=0, concat_axis=0, tiled=True)

    arrived_g = outward(part_g)
    arrived_i = outward(part_i)
    mh = MX // dp

    if jl == MY and xl == 8:
        step = 4
        spec_shape = (dp, C, mh, 2 * MY)
        spec_g, along = pl.pallas_call(
            functools.partial(modes_kernel, dp=dp, step=step),
            grid=(MX // step,),
            in_specs=[
                whole(arrived_g.shape),
                pl.BlockSpec((step, kl, 2 * C * C), lambda m: (m, 0, 0)),
                whole(t["xf"].shape),
                whole(t["xi"].shape),
                whole(t["eo"].shape),
            ],
            out_specs=[whole(spec_shape), whole(arrived_g.shape)],
            out_shape=[
                jax.ShapeDtypeStruct(spec_shape, F32),
                jax.ShapeDtypeStruct(arrived_g.shape, F32),
            ],
            scratch_shapes=[pltpu.VMEM((C * MX, 2 * MY), F32)],
            compiler_params=params(),
            cost_estimate=cost(1e9, spectral_weight.size * 4 + arrived_g.size * 8),
            name="modes",
        )(arrived_g, spectral_weight, t["xf"], t["xi"], t["eo"])
        spec_i = pl.pallas_call(
            functools.partial(spectrum_kernel, dp=dp),
            in_specs=[whole(arrived_i.shape), whole(t["xf"].shape)],
            out_specs=whole(spec_shape),
            out_shape=jax.ShapeDtypeStruct(spec_shape, F32),
            grid=(1,),
            compiler_params=params(),
            cost_estimate=cost(1e8, arrived_i.size * 5),
            name="spectrum",
        )(arrived_i, t["xf"])
        both_g = lax.all_to_all(spec_g, "dp", split_axis=0, concat_axis=0, tiled=True)
        both_i = lax.all_to_all(spec_i, "dp", split_axis=0, concat_axis=0, tiled=True)
        wstep = 2
        weight_grad = pl.pallas_call(
            functools.partial(weight_kernel, dp=dp, step=wstep),
            grid=(mh // wstep,),
            in_specs=[whole(spec_shape), whole(spec_shape)]
            + [whole(t["eo"].shape), whole(t["ei"].shape)],
            out_specs=pl.BlockSpec((wstep, kl, 2 * C * C), lambda m: (m, 0, 0)),
            out_shape=jax.ShapeDtypeStruct((mh, kl, 2 * C * C), F32),
            compiler_params=params(),
            cost_estimate=cost(1e9, mh * kl * 2 * C * C * 4),
            name="weight_grad",
        )(both_g, both_i, t["eo"], t["ei"])
    else:
        weight_grad, along = modes_plain(space, dp, arrived_g, arrived_i, spectral_weight, jl)

    back = lax.all_to_all(along, "space", split_axis=0, concat_axis=0, tiled=True)
    back = back.reshape(MZ, q, xl, C, 2, jl).transpose(0, 2, 3, 4, 1, 5).reshape(MZ, xl, C, 2 * MY)
    kron = jnp.kron(skip_weight.T, jnp.eye(8, dtype=F32))
    input_grad = pl.pallas_call(
        inverse_kernel,
        grid=(xl,),
        in_specs=[lines, plane, whole(kron.shape), whole(t["yi"].shape), whole(t["zi"].shape)],
        out_specs=plane,
        out_shape=field,
        scratch_shapes=[pltpu.VMEM((MZ * C, N), F32)] * 2,
        compiler_params=params(),
        cost_estimate=cost(nbytes * 600, nbytes * 2),
        name="inverse",
    )(back, gp, kron, t["yi"], t["zi"])
    return input_grad, weight_grad, skip_grad


def modes_plain(space, dp, arrived_g, arrived_i, weights, jl):
    cx, sx = waves(signed(MX))
    fwd = jnp.asarray(np.stack([np.stack([cx.T, -sx.T], 1), np.stack([sx.T, cx.T], 1)], 0), F32)
    inv = jnp.asarray(np.stack([np.stack([cx, sx], 1), np.stack([-sx, cx], 1)], 0), F32)
    ein = functools.partial(jnp.einsum, precision=lax.Precision.HIGHEST)

    def spectrum(a):
        return ein("xcrj,rxsm->scmj", a.reshape(N, C, 2, jl), fwd) * NORM

    g, i = spectrum(arrived_g), spectrum(arrived_i)

    def other(s):
        return lax.all_to_all(s[None], "dp", split_axis=3, concat_axis=0, tiled=True)

    bg, bi = other(g), other(i)
    real = ein("bomk,bimk->mkoi", bg[:, 0], bi[:, 0]) + ein("bomk,bimk->mkoi", bg[:, 1], bi[:, 1])
    imag = ein("bomk,bimk->mkoi", bg[:, 1], bi[:, 0]) - ein("bomk,bimk->mkoi", bg[:, 0], bi[:, 1])
    weight_grad = jnp.stack([real, imag], 2).reshape(MX // dp, jl, 2 * C * C)
    w = weights.reshape(MX, jl, 2, C, C)
    dr = ein("mkoi,omk->imk", w[:, :, 0], g[0]) + ein("mkoi,omk->imk", w[:, :, 1], g[1])
    di = ein("mkoi,omk->imk", w[:, :, 0], g[1]) - ein("mkoi,omk->imk", w[:, :, 1], g[0])
    along = ein("rimk,rmsx->xisk", jnp.stack([dr, di], 0), inv) * NORM
    return weight_grad, along.reshape(arrived_g.shape)


def solution(mesh):
    in_specs = (
        P("dp", None, "space", None, None),
        P("dp", None, "space", None, None),
        P("dp", None, "space", None, None),
        P(None, "space", None),
        P(),
    )
    out_specs = (P("dp", None, "space", None, None), P("dp", "space", None), P())
    local = functools.partial(body, mesh.shape["space"], mesh.shape["dp"])
    return jax.shard_map(local, mesh=mesh, in_specs=in_specs, out_specs=out_specs, check_vma=False)
```

```python
import functools

import jax
import jax.numpy as jnp
import ml_dtypes
import numpy as np
from jax import lax
from jax.experimental import pallas as pl
from jax.experimental.pallas import tpu as pltpu
from jax.sharding import PartitionSpec as P

N = 128
C = 32
MX = 32
MY = 64
MZ = 16
NORM = float(N) ** -1.5

tanh_scale = 0.7978845608028654
cubic_term = 0.044715
BF = jnp.bfloat16
F32 = jnp.float32
LIMIT = 48 * 1024 * 1024
FUSED_LIMIT = 60 * 1024 * 1024


def signed(count):
    p = np.arange(count)
    return np.where(p < count // 2, p, p - count)


def waves(freq):
    angle = 2 * np.pi / N * np.mod(freq[:, None] * np.arange(N)[None, :], N)
    return np.cos(angle), np.sin(angle)


def halves(table):
    hi = table.astype(np.float32).astype(ml_dtypes.bfloat16)
    lo = (table - hi.astype(np.float64)).astype(np.float32).astype(ml_dtypes.bfloat16)
    return hi, lo


def make_tables():
    cx, sx = waves(signed(MX))
    cy, sy = waves(signed(MY))
    cz, sz = waves(np.arange(MZ))
    t = {}
    t["zf"] = np.concatenate(halves(np.concatenate([cz, -sz], 0)), 0)
    hi, lo = halves(np.block([[cy.T, -sy.T], [sy.T, cy.T]]))
    t["yf"] = np.concatenate([hi, hi, lo], 0)
    hi, lo = halves(np.concatenate([cx, sx], 0))
    t["xf"] = np.concatenate([hi, lo, hi], 1)
    t["xi"] = np.concatenate([hi.T, lo.T, hi.T], 1)
    hi, lo = halves(np.block([[cy, sy], [-sy, cy]]))
    t["yi"] = np.concatenate([hi, hi, lo], 0)
    hi, lo = halves(np.concatenate([cz, -sz], 0))
    t["zi"] = np.concatenate([hi, hi, lo], 0)
    eye = np.eye(C)
    spread_out = np.repeat(eye, C, axis=1)
    spread_in = np.tile(eye, (1, C))
    t["eo"] = np.concatenate([spread_out, spread_out], 0).astype(ml_dtypes.bfloat16)
    t["ei"] = np.concatenate([spread_in, spread_in], 0).astype(ml_dtypes.bfloat16)
    return t


def split(x):
    hi = x.astype(BF)
    lo = (x - hi.astype(F32)).astype(BF)
    return hi, lo


def nn(a, b):
    return lax.dot_general(a, b, (((1,), (0,)), ((), ())), preferred_element_type=F32)


def nt(a, b):
    return lax.dot_general(a, b, (((1,), (1,)), ((), ())), preferred_element_type=F32)


def tn(a, b):
    return lax.dot_general(a, b, (((0,), (0,)), ((), ())), preferred_element_type=F32)


def gelu_slope(h):
    t = jnp.tanh(tanh_scale * (h + cubic_term * h * h * h))
    return 0.5 * (1.0 + t) + 0.5 * h * (1.0 - t * t) * tanh_scale * (1.0 + 3.0 * cubic_term * h * h)


GROUP = 8


def planes_forward(d, first, zf_ref, yf_ref, out2d):
    hi, lo = split(d.reshape(GROUP * N, N))
    a = nt(zf_ref[...], hi)
    z = a[: 2 * MZ] + a[2 * MZ :] + nt(zf_ref[: 2 * MZ, :], lo)
    rows = []
    for c in range(GROUP):
        cols = slice(c * N, (c + 1) * N)
        rows.append(jnp.concatenate([z[:MZ, cols], z[MZ:, cols]], 1))
    hi, lo = split(jnp.concatenate(rows, 0))
    y = nn(jnp.concatenate([hi, lo, hi], 1), yf_ref[...])
    for c in range(GROUP):
        out2d[pl.ds(first + c, MZ, stride=C), :] = y[c * MZ : (c + 1) * MZ, :]


def grad_kernel(pre_ref, cot_ref, zf_ref, yf_ref, gp_ref, out_ref):
    out2d = out_ref.reshape(MZ * C, 2 * MY)
    for g in range(0, C, GROUP):
        gp = cot_ref[0, g : g + GROUP, 0] * gelu_slope(pre_ref[0, g : g + GROUP, 0])
        gp_ref[0, g : g + GROUP, 0] = gp
        planes_forward(gp, g, zf_ref, yf_ref, out2d)


def input_kernel(in_ref, gp_ref, zf_ref, yf_ref, out_ref, acc_ref):
    out2d = out_ref.reshape(MZ * C, 2 * MY)

    @pl.when(pl.program_id(0) == 0)
    def _():
        acc_ref[...] = jnp.zeros_like(acc_ref)

    for g in range(0, C, GROUP):
        planes_forward(in_ref[0, g : g + GROUP, 0], g, zf_ref, yf_ref, out2d)

    def rows(ref, y):
        a = ref[0, :, 0, pl.ds(y, 8), :].reshape(C * 8, N)
        b = ref[0, :, 0, pl.ds(y + 8, 8), :].reshape(C * 8, N)
        return split(jnp.concatenate([a, b], 1))

    @pl.loop(0, N // 16)
    def _(s):
        y = pl.multiple_of(s * 16, 16)
        gh, gl = rows(gp_ref, y)
        ih, il = rows(in_ref, y)
        acc_ref[...] += nt(
            jnp.concatenate([gh, gl, gh], 1), jnp.concatenate([ih, ih, il], 1)
        )


def fold(x):
    total = x[:, :128]
    for t in range(1, C * C // 128):
        total = total + x[:, t * 128 : (t + 1) * 128]
    return total


def swap(x):
    return pltpu.roll(x, MY, 1)


def lane_sign(rows, first):
    lane = lax.broadcasted_iota(jnp.int32, (rows, 2 * MY), 1)
    return jnp.where(lane < MY, first, -first).astype(F32)


def x_forward(a2d, xf_ref):
    for c in range(C):
        hi, lo = split(a2d[pl.ds(c, N, stride=C), :])
        p = nn(xf_ref[...], jnp.concatenate([hi, hi, lo], 0))
        s = (p[:MX] + lane_sign(MX, 1.0) * swap(p[MX:])) * NORM
        yield c, s


def modes_kernel(a_ref, w_ref, xf_ref, xi_ref, eo_ref, s_ref, out_ref, d_ref, *, dp, step):
    mh = MX // dp
    a2d = a_ref.reshape(N * C, 2 * MY)
    s2d = s_ref.reshape(MX * C, 2 * MY)
    out2d = out_ref.reshape(N * C, 2 * MY)
    pid = pl.program_id(0)

    @pl.when(pid == 0)
    def _():
        for c, s in x_forward(a2d, xf_ref):
            for h in range(dp):
                s_ref[h, c] = s[h * mh : (h + 1) * mh]

    for u in range(step):
        m = pid * step + u
        start = (m // mh) * (C * mh) + m % mh
        hi, lo = split(s2d[pl.ds(start, C, stride=mh), :])
        g = tn(jnp.concatenate([hi, lo], 0), eo_ref[...])
        gr, gi = g[:MY], g[MY:]
        wr, wi = w_ref[u, :, : C * C], w_ref[u, :, C * C :]

        both = jnp.concatenate([fold(wr * gr + wi * gi), fold(wr * gi - wi * gr)], 0).T
        total = both[:C] + both[C : 2 * C] + both[2 * C : 3 * C] + both[3 * C :]
        d_ref[pl.ds(m, C, stride=MX), :] = total * NORM

    @pl.when(pid == MX // step - 1)
    def _():
        for i in range(C):
            d = d_ref[i * MX : (i + 1) * MX, :]
            hi, lo = split(jnp.concatenate([d, lane_sign(MX, -1.0) * swap(d)], 0))
            out2d[pl.ds(i, N, stride=C), :] = nn(xi_ref[...], jnp.concatenate([hi, hi, lo], 0))


def spectrum_kernel(a_ref, xf_ref, s_ref, *, dp):
    mh = MX // dp
    a2d = a_ref.reshape(N * C, 2 * MY)
    for c, s in x_forward(a2d, xf_ref):
        for h in range(dp):
            s_ref[h, c] = s[h * mh : (h + 1) * mh]


def weight_kernel(g_ref, i_ref, eo_ref, ei_ref, out_ref, *, dp, step):
    mh = MX // dp
    g2d = g_ref.reshape(MX * C, 2 * MY)
    i2d = i_ref.reshape(MX * C, 2 * MY)
    for u in range(step):
        m = pl.program_id(0) * step + u
        real = imag = None
        for b in range(dp):
            at = pl.ds(b * (C * mh) + m, C, stride=mh)
            g = tn(jnp.concatenate(split(g2d[at, :]), 0), eo_ref[...])
            i = tn(jnp.concatenate(split(i2d[at, :]), 0), ei_ref[...])
            gr, gi, ir, ii = g[:MY], g[MY:], i[:MY], i[MY:]
            r = gr * ir + gi * ii
            j = gi * ir - gr * ii
            real, imag = (r, j) if real is None else (real + r, imag + j)
        out_ref[u, :, : C * C] = real
        out_ref[u, :, C * C :] = imag


def inverse_kernel(b_ref, gp_ref, k_ref, yi_ref, zi_ref, out_ref, re_ref, im_ref):
    hi, lo = split(b_ref.reshape(MZ * C, 2 * MY)[...])
    v = nn(jnp.concatenate([hi, lo, hi], 1), yi_ref[...])
    re_ref[...] = v[:, :N]
    im_ref[...] = v[:, N:]
    for i in range(C):
        at = pl.ds(i, MZ, stride=C)
        hi, lo = split(jnp.concatenate([re_ref[at, :], im_ref[at, :]], 0))
        out_ref[0, i, 0] = tn(jnp.concatenate([hi, lo, hi], 0), zi_ref[...])
    kh, kl = split(k_ref[...])
    k3 = jnp.concatenate([kh, kl, kh], 1)

    @pl.loop(0, N // 16)
    def _(s):
        y = pl.multiple_of(s * 16, 16)
        a = gp_ref[0, :, 0, pl.ds(y, 8), :].reshape(C * 8, N)
        b = gp_ref[0, :, 0, pl.ds(y + 8, 8), :].reshape(C * 8, N)
        gh, gl = split(jnp.concatenate([a, b], 1))
        r = nn(k3, jnp.concatenate([gh, gh, gl], 0))
        out_ref[0, :, 0, pl.ds(y, 8), :] += r[:, :N].reshape(C, 8, N)
        out_ref[0, :, 0, pl.ds(y + 8, 8), :] += r[:, N:].reshape(C, 8, N)


def whole(shape):
    return pl.BlockSpec(shape, lambda *_: (0,) * len(shape))


def params():
    return pltpu.CompilerParams(vmem_limit_bytes=LIMIT)


def cost(flops, nbytes):
    return pl.CostEstimate(flops=int(flops), bytes_accessed=int(nbytes), transcendentals=0)


def body(space, dp, inputs, preact, cotangent, spectral_weight, skip_weight):
    t = {k: jnp.asarray(v) for k, v in make_tables().items()}
    xl = inputs.shape[2]
    kl = spectral_weight.shape[1]
    field = jax.ShapeDtypeStruct(inputs.shape, F32)
    spread = jax.ShapeDtypeStruct((MZ, xl, C, 2 * MY), F32)
    plane = pl.BlockSpec((1, C, 1, N, N), lambda x: (0, 0, x, 0, 0))
    lines = pl.BlockSpec((MZ, 1, C, 2 * MY), lambda x: (0, x, 0, 0))
    nbytes = inputs.size * 4

    gp, part_g = pl.pallas_call(
        grad_kernel,
        grid=(xl,),
        in_specs=[plane, plane, whole(t["zf"].shape), whole(t["yf"].shape)],
        out_specs=[plane, lines],
        out_shape=[field, spread],
        compiler_params=params(),
        cost_estimate=cost(nbytes * 300, nbytes * 4),
        name="grad_forward",
    )(preact, cotangent, t["zf"], t["yf"])
    part_i, acc = pl.pallas_call(
        input_kernel,
        grid=(xl,),
        in_specs=[plane, plane, whole(t["zf"].shape), whole(t["yf"].shape)],
        out_specs=[lines, whole((C * 8, C * 8))],
        out_shape=[spread, jax.ShapeDtypeStruct((C * 8, C * 8), F32)],
        compiler_params=params(),
        cost_estimate=cost(nbytes * 600, nbytes * 3),
        name="input_forward",
    )(inputs, gp, t["zf"], t["yf"])
    diag = jnp.einsum("oyiy->oi", acc.reshape(C, 8, C, 8), precision=lax.Precision.HIGHEST)
    skip_grad = lax.psum(NORM * diag, ("dp", "space"))

    q = space // MZ
    jl = MY // q

    def outward(part):
        p = part.reshape(MZ, xl, C, 2, q, jl).transpose(0, 4, 1, 2, 3, 5)
        p = p.reshape(space, xl, C, 2 * jl)
        return lax.all_to_all(p, "space", split_axis=0, concat_axis=0, tiled=True)

    arrived_g = outward(part_g)
    arrived_i = outward(part_i)
    mh = MX // dp

    if jl == MY and xl == 8:
        step = 4
        spec_shape = (dp, C, mh, 2 * MY)
        spec_g, along = pl.pallas_call(
            functools.partial(modes_kernel, dp=dp, step=step),
            grid=(MX // step,),
            in_specs=[
                whole(arrived_g.shape),
                pl.BlockSpec((step, kl, 2 * C * C), lambda m: (m, 0, 0)),
                whole(t["xf"].shape),
                whole(t["xi"].shape),
                whole(t["eo"].shape),
            ],
            out_specs=[whole(spec_shape), whole(arrived_g.shape)],
            out_shape=[
                jax.ShapeDtypeStruct(spec_shape, F32),
                jax.ShapeDtypeStruct(arrived_g.shape, F32),
            ],
            scratch_shapes=[pltpu.VMEM((C * MX, 2 * MY), F32)],
            compiler_params=params(),
            cost_estimate=cost(1e9, spectral_weight.size * 4 + arrived_g.size * 8),
            name="modes",
        )(arrived_g, spectral_weight, t["xf"], t["xi"], t["eo"])
        spec_i = pl.pallas_call(
            functools.partial(spectrum_kernel, dp=dp),
            in_specs=[whole(arrived_i.shape), whole(t["xf"].shape)],
            out_specs=whole(spec_shape),
            out_shape=jax.ShapeDtypeStruct(spec_shape, F32),
            grid=(1,),
            compiler_params=params(),
            cost_estimate=cost(1e8, arrived_i.size * 5),
            name="spectrum",
        )(arrived_i, t["xf"])
        both_g = lax.all_to_all(spec_g, "dp", split_axis=0, concat_axis=0, tiled=True)
        both_i = lax.all_to_all(spec_i, "dp", split_axis=0, concat_axis=0, tiled=True)
        wstep = 2
        weight_grad = pl.pallas_call(
            functools.partial(weight_kernel, dp=dp, step=wstep),
            grid=(mh // wstep,),
            in_specs=[whole(spec_shape), whole(spec_shape)]
            + [whole(t["eo"].shape), whole(t["ei"].shape)],
            out_specs=pl.BlockSpec((wstep, kl, 2 * C * C), lambda m: (m, 0, 0)),
            out_shape=jax.ShapeDtypeStruct((mh, kl, 2 * C * C), F32),
            compiler_params=params(),
            cost_estimate=cost(1e9, mh * kl * 2 * C * C * 4),
            name="weight_grad",
        )(both_g, both_i, t["eo"], t["ei"])
    else:
        weight_grad, along = modes_plain(space, dp, arrived_g, arrived_i, spectral_weight, jl)

    back = lax.all_to_all(along, "space", split_axis=0, concat_axis=0, tiled=True)
    back = back.reshape(MZ, q, xl, C, 2, jl).transpose(0, 2, 3, 4, 1, 5).reshape(MZ, xl, C, 2 * MY)
    kron = jnp.kron(skip_weight.T, jnp.eye(8, dtype=F32))
    input_grad = pl.pallas_call(
        inverse_kernel,
        grid=(xl,),
        in_specs=[lines, plane, whole(kron.shape), whole(t["yi"].shape), whole(t["zi"].shape)],
        out_specs=plane,
        out_shape=field,
        scratch_shapes=[pltpu.VMEM((MZ * C, N), F32)] * 2,
        compiler_params=params(),
        cost_estimate=cost(nbytes * 600, nbytes * 2),
        name="inverse",
    )(back, gp, kron, t["yi"], t["zi"])
    return input_grad, weight_grad, skip_grad


def modes_plain(space, dp, arrived_g, arrived_i, weights, jl):
    cx, sx = waves(signed(MX))
    fwd = jnp.asarray(np.stack([np.stack([cx.T, -sx.T], 1), np.stack([sx.T, cx.T], 1)], 0), F32)
    inv = jnp.asarray(np.stack([np.stack([cx, sx], 1), np.stack([-sx, cx], 1)], 0), F32)
    ein = functools.partial(jnp.einsum, precision=lax.Precision.HIGHEST)

    def spectrum(a):
        return ein("xcrj,rxsm->scmj", a.reshape(N, C, 2, jl), fwd) * NORM

    g, i = spectrum(arrived_g), spectrum(arrived_i)

    def other(s):
        return lax.all_to_all(s[None], "dp", split_axis=3, concat_axis=0, tiled=True)

    bg, bi = other(g), other(i)
    real = ein("bomk,bimk->mkoi", bg[:, 0], bi[:, 0]) + ein("bomk,bimk->mkoi", bg[:, 1], bi[:, 1])
    imag = ein("bomk,bimk->mkoi", bg[:, 1], bi[:, 0]) - ein("bomk,bimk->mkoi", bg[:, 0], bi[:, 1])
    weight_grad = jnp.stack([real, imag], 2).reshape(MX // dp, jl, 2 * C * C)
    w = weights.reshape(MX, jl, 2, C, C)
    dr = ein("mkoi,omk->imk", w[:, :, 0], g[0]) + ein("mkoi,omk->imk", w[:, :, 1], g[1])
    di = ein("mkoi,omk->imk", w[:, :, 0], g[1]) - ein("mkoi,omk->imk", w[:, :, 1], g[0])
    along = ein("rimk,rmsx->xisk", jnp.stack([dr, di], 0), inv) * NORM
    return weight_grad, along.reshape(arrived_g.shape)


def selector(rows):
    row = lax.broadcasted_iota(jnp.int32, (rows, 8 * C), 0)
    col = lax.broadcasted_iota(jnp.int32, (rows, 8 * C), 1)
    return jnp.where(col // 8 == row, 1.0, 0.0).astype(BF)


def same_row():
    row = lax.broadcasted_iota(jnp.int32, (8 * C, 8 * C), 0)
    col = lax.broadcasted_iota(jnp.int32, (8 * C, 8 * C), 1)
    return row % 8 == col % 8


def fused_kernel(
    pre_ref, cot_ref, in_ref, w_ref, sw_ref, zf_ref, yf_ref, xf_ref, xi_ref, eo_ref,
    skip_ref, spec_ref, sum_ref, back_ref,
    gp_ref, k_ref, acc_ref, sg_ref, si_ref, sb_ref, rg_ref, ri_ref, d_ref, ss_ref, rs_ref,
    send_g, send_i, send_b, send_s, recv_g, recv_i, recv_b, recv_s, local,
    *, space, dp, xl, wstep,
):
    step = pl.program_id(0)
    me = lax.axis_index("space")
    half = lax.axis_index("dp")
    mh = MX // dp
    msteps = MX // wstep

    def others(action):
        @pl.loop(1, space)
        def _(r):
            action(lax.rem(me + r, space))

    def put(src, dst, send, recv, target):
        pltpu.make_async_remote_copy(
            src_ref=src, dst_ref=dst, send_sem=send, recv_sem=recv,
            device_id={"space": target}, device_id_type=pl.DeviceIdType.MESH,
        ).start()

    def await_all(ref, sem):
        part = ref.at[pl.ds(0, space - 1)]
        pltpu.make_async_copy(part, part, sem).wait()

    @pl.when(step == 0)
    def _():
        barrier = pltpu.get_barrier_semaphore()

        def greet(target):
            pl.semaphore_signal(
                barrier, inc=1, device_id={"space": target}, device_id_type=pl.DeviceIdType.MESH
            )

        others(greet)
        pl.semaphore_wait(barrier, space - 1)
        acc_ref[...] = jnp.zeros_like(acc_ref)
        sel = selector(C)
        pieces = []
        for piece in split(sw_ref[...]):
            wide = tn(piece, sel).astype(BF)
            pieces.append(jnp.where(same_row(), tn(sel, wide), 0.0).astype(BF))
        k_ref[...] = jnp.concatenate([pieces[0], pieces[1], pieces[0]], 1)

    @pl.when(step < xl)
    def _():
        x = step
        out2d = sg_ref.at[x].reshape(MZ * C, 2 * MY)
        for g in range(0, C, GROUP):
            gp = cot_ref[0, g : g + GROUP, 0] * gelu_slope(pre_ref[0, g : g + GROUP, 0])
            gp_ref[x, g : g + GROUP] = gp
            planes_forward(gp, g, zf_ref, yf_ref, out2d)
        rg_ref[me, x] = sg_ref[x, me]
        others(lambda t: put(sg_ref.at[x, t], rg_ref.at[me, x], send_g, recv_g, t))

    @pl.when((step >= xl) & (step < 2 * xl))
    def _():
        x = step - xl
        out2d = si_ref.at[x].reshape(MZ * C, 2 * MY)
        for g in range(0, C, GROUP):
            planes_forward(in_ref[0, g : g + GROUP, 0], g, zf_ref, yf_ref, out2d)
        ri_ref[me, x] = si_ref[x, me]
        others(lambda t: put(si_ref.at[x, t], ri_ref.at[me, x], send_i, recv_i, t))

        @pl.loop(0, N // 16)
        def _(s):
            y = pl.multiple_of(s * 16, 16)
            ga = gp_ref[x, :, pl.ds(y, 8), :].reshape(C * 8, N)
            gb = gp_ref[x, :, pl.ds(y + 8, 8), :].reshape(C * 8, N)
            gh, gl = split(jnp.concatenate([ga, gb], 1))
            ia = in_ref[0, :, 0, pl.ds(y, 8), :].reshape(C * 8, N)
            ib = in_ref[0, :, 0, pl.ds(y + 8, 8), :].reshape(C * 8, N)
            ih, il = split(jnp.concatenate([ia, ib], 1))
            acc_ref[...] += nt(
                jnp.concatenate([gh, gl, gh], 1), jnp.concatenate([ih, ih, il], 1)
            )
            r = nn(k_ref[...], jnp.concatenate([gh, gh, gl], 0))
            skip_ref[0, :, 0, pl.ds(y, 8), :] = r[:, :N].reshape(C, 8, N)
            skip_ref[0, :, 0, pl.ds(y + 8, 8), :] = r[:, N:].reshape(C, 8, N)

    @pl.when(step == 2 * xl - 1)
    def _():
        hi, lo = split(jnp.where(same_row(), acc_ref[...], 0.0))
        sel = selector(C)
        hi, lo = split(nn(sel, hi) + nn(sel, lo))
        wide = selector(128)
        ss_ref[...] = nt(hi, wide) + nt(lo, wide)
        rs_ref[me] = ss_ref[...]
        others(lambda t: put(ss_ref, rs_ref.at[me], send_s, recv_s, t))

    s2d = spec_ref.reshape(dp * 2 * C * mh, 2 * MY)

    @pl.when(step == 2 * xl)
    def _():
        await_all(rg_ref, recv_g)
        await_all(rg_ref, send_g)
        for c, s in x_forward(rg_ref.reshape(N * C, 2 * MY), xf_ref):
            for h in range(dp):
                spec_ref[lax.rem(h + half, dp), 0, c] = s[h * mh : (h + 1) * mh]

    @pl.when(step >= 2 * xl)
    def _():
        for u in range(wstep):
            m = (step - 2 * xl) * wstep + u
            slot = lax.rem(m // mh + half, dp)
            start = slot * (2 * C * mh) + lax.rem(m, mh)
            hi, lo = split(s2d[pl.ds(start, C, stride=mh), :])
            g = tn(jnp.concatenate([hi, lo], 0), eo_ref[...])
            gr, gi = g[:MY], g[MY:]
            wr, wi = w_ref[u, :, : C * C], w_ref[u, :, C * C :]
            both = jnp.concatenate([fold(wr * gr + wi * gi), fold(wr * gi - wi * gr)], 0).T
            total = both[:C] + both[C : 2 * C] + both[2 * C : 3 * C] + both[3 * C :]
            d_ref[pl.ds(m, C, stride=MX), :] = total * NORM

    @pl.when(step == 2 * xl + msteps - 1)
    def _():
        out2d = sb_ref.reshape(N * C, 2 * MY)
        for i in range(C):
            d = d_ref[i * MX : (i + 1) * MX, :]
            hi, lo = split(jnp.concatenate([d, lane_sign(MX, -1.0) * swap(d)], 0))
            out2d[pl.ds(i, N, stride=C), :] = nn(xi_ref[...], jnp.concatenate([hi, hi, lo], 0))
        own = pltpu.make_async_copy(sb_ref.at[me], back_ref.at[me], local)
        own.start()
        others(lambda t: put(sb_ref.at[t], back_ref.at[me], send_b, recv_b, t))
        await_all(rs_ref, recv_s)
        await_all(rs_ref, send_s)
        total = rs_ref[0]
        for r in range(1, space):
            total = total + rs_ref[r]
        sum_ref[...] = total
        await_all(ri_ref, recv_i)
        await_all(ri_ref, send_i)
        for c, s in x_forward(ri_ref.reshape(N * C, 2 * MY), xf_ref):
            for h in range(dp):
                spec_ref[lax.rem(h + half, dp), 1, c] = s[h * mh : (h + 1) * mh]
        own.wait()
        await_all(sb_ref, send_b)
        await_all(sb_ref, recv_b)


def pair_weight_kernel(mine_ref, other_ref, eo_ref, ei_ref, out_ref, *, step):
    rows = mine_ref.shape[1] * mine_ref.shape[2] * mine_ref.shape[3]
    mh = mine_ref.shape[3]
    half = rows // 2
    for u in range(step):
        m = pl.program_id(0) * step + u
        real = imag = None
        for ref in (mine_ref, other_ref):
            flat = ref.reshape(rows, 2 * MY)
            gs = flat[pl.ds(m, C, stride=mh), :]
            vs = flat[pl.ds(half + m, C, stride=mh), :]
            g = tn(jnp.concatenate(split(gs), 0), eo_ref[...])
            i = tn(jnp.concatenate(split(vs), 0), ei_ref[...])
            gr, gi, ir, ii = g[:MY], g[MY:], i[:MY], i[MY:]
            r = gr * ir + gi * ii
            j = gi * ir - gr * ii
            real, imag = (r, j) if real is None else (real + r, imag + j)
        out_ref[u, :, : C * C] = real
        out_ref[u, :, C * C :] = imag


def restore_kernel(b_ref, sk_ref, yi_ref, zi_ref, out_ref, re_ref, im_ref):
    hi, lo = split(b_ref.reshape(MZ * C, 2 * MY)[...])
    v = nn(jnp.concatenate([hi, lo, hi], 1), yi_ref[...])
    re_ref[...] = v[:, :N]
    im_ref[...] = v[:, N:]
    for i in range(C):
        at = pl.ds(i, MZ, stride=C)
        hi, lo = split(jnp.concatenate([re_ref[at, :], im_ref[at, :]], 0))
        out_ref[0, i, 0] = sk_ref[0, i, 0] + tn(jnp.concatenate([hi, lo, hi], 0), zi_ref[...])


def fused_body(space, dp, inputs, preact, cotangent, spectral_weight, skip_weight):
    t = {k: jnp.asarray(v) for k, v in make_tables().items()}
    xl = inputs.shape[2]
    kl = spectral_weight.shape[1]
    mh = MX // dp
    field = jax.ShapeDtypeStruct(inputs.shape, F32)
    wstep = 4
    last = MX // wstep - 1
    nbytes = inputs.size * 4

    def plane(first):
        return pl.BlockSpec((1, C, 1, N, N), lambda s: (0, 0, jnp.clip(s - first, 0, xl - 1), 0, 0))

    arrive = (space, xl, C, 2 * MY)
    send = (xl, space, C, 2 * MY)
    spec_shape = (dp, 2, C, mh, 2 * MY)
    dma = pltpu.SemaphoreType.DMA
    skip_term, spec, summed, back = pl.pallas_call(
        functools.partial(fused_kernel, space=space, dp=dp, xl=xl, wstep=wstep),
        grid=(2 * xl + MX // wstep,),
        in_specs=[
            plane(0),
            plane(0),
            plane(xl),
            pl.BlockSpec(
                (wstep, kl, 2 * C * C), lambda s: (jnp.clip(s - 2 * xl, 0, last), 0, 0)
            ),
            whole(skip_weight.shape),
            whole(t["zf"].shape),
            whole(t["yf"].shape),
            whole(t["xf"].shape),
            whole(t["xi"].shape),
            whole(t["eo"].shape),
        ],
        out_specs=[
            plane(xl),
            whole(spec_shape),
            whole((C, 128)),
            pl.BlockSpec(memory_space=pl.ANY),
        ],
        out_shape=[
            field,
            jax.ShapeDtypeStruct(spec_shape, F32),
            jax.ShapeDtypeStruct((C, 128), F32),
            jax.ShapeDtypeStruct(arrive, F32),
        ],
        scratch_shapes=[
            pltpu.VMEM((xl, C, N, N), F32),
            pltpu.VMEM((8 * C, 24 * C), BF),
            pltpu.VMEM((8 * C, 8 * C), F32),
            pltpu.VMEM(send, F32),
            pltpu.VMEM(send, F32),
            pltpu.VMEM(arrive, F32),
            pltpu.VMEM(arrive, F32),
            pltpu.VMEM(arrive, F32),
            pltpu.VMEM((C * MX, 2 * MY), F32),
            pltpu.VMEM((C, 128), F32),
            pltpu.VMEM((space, C, 128), F32),
        ]
        + [dma] * 9,
        compiler_params=pltpu.CompilerParams(
            vmem_limit_bytes=FUSED_LIMIT, collective_id=0, has_side_effects=True
        ),
        cost_estimate=cost(nbytes * 1500, nbytes * 5),
        name="fused_forward",
    )(
        preact, cotangent, inputs, spectral_weight, skip_weight,
        t["zf"], t["yf"], t["xf"], t["xi"], t["eo"],
    )
    pairs = [(0, 1), (1, 0)]
    theirs = lax.ppermute(spec[1:], "dp", pairs)
    skip_grad = NORM * (summed + lax.ppermute(summed, "dp", pairs))[:, :C]
    input_grad = pl.pallas_call(
        restore_kernel,
        grid=(xl,),
        in_specs=[
            pl.BlockSpec((MZ, 1, C, 2 * MY), lambda x: (0, x, 0, 0)),
            pl.BlockSpec((1, C, 1, N, N), lambda x: (0, 0, x, 0, 0)),
            whole(t["yi"].shape),
            whole(t["zi"].shape),
        ],
        out_specs=pl.BlockSpec((1, C, 1, N, N), lambda x: (0, 0, x, 0, 0)),
        out_shape=field,
        scratch_shapes=[pltpu.VMEM((MZ * C, N), F32)] * 2,
        compiler_params=params(),
        cost_estimate=cost(nbytes * 300, nbytes * 2),
        name="inverse",
    )(back, skip_term, t["yi"], t["zi"])
    step = 2
    half_shape = (1,) + spec_shape[1:]
    weight_grad = pl.pallas_call(
        functools.partial(pair_weight_kernel, step=step),
        grid=(mh // step,),
        in_specs=[
            whole(half_shape),
            whole(half_shape),
            whole(t["eo"].shape),
            whole(t["ei"].shape),
        ],
        out_specs=pl.BlockSpec((step, kl, 2 * C * C), lambda m: (m, 0, 0)),
        out_shape=jax.ShapeDtypeStruct((mh, kl, 2 * C * C), F32),
        compiler_params=params(),
        cost_estimate=cost(1e9, mh * kl * 2 * C * C * 4),
        name="weight_grad",
    )(spec[:1], theirs, t["eo"], t["ei"])
    return input_grad, weight_grad, skip_grad


def solution(mesh):
    in_specs = (
        P("dp", None, "space", None, None),
        P("dp", None, "space", None, None),
        P("dp", None, "space", None, None),
        P(None, "space", None),
        P(),
    )
    out_specs = (P("dp", None, "space", None, None), P("dp", "space", None), P())
    space, dp = mesh.shape["space"], mesh.shape["dp"]
    form = fused_body if space == MZ and dp == 2 else body
    local = functools.partial(form, space, dp)
    return jax.shard_map(local, mesh=mesh, in_specs=in_specs, out_specs=out_specs, check_vma=False)
```

```python
import functools

import jax
import jax.numpy as jnp
import ml_dtypes
import numpy as np
from jax import lax
from jax.experimental import pallas as pl
from jax.experimental.pallas import tpu as pltpu
from jax.sharding import PartitionSpec as P

N = 128
C = 32
MX = 32
MY = 64
MZ = 16
NORM = float(N) ** -1.5

tanh_scale = 0.7978845608028654
cubic_term = 0.044715
BF = jnp.bfloat16
F32 = jnp.float32
LIMIT = 48 * 1024 * 1024
FUSED_LIMIT = 60 * 1024 * 1024


def signed(count):
    p = np.arange(count)
    return np.where(p < count // 2, p, p - count)


def waves(freq):
    angle = 2 * np.pi / N * np.mod(freq[:, None] * np.arange(N)[None, :], N)
    return np.cos(angle), np.sin(angle)


def halves(table):
    hi = table.astype(np.float32).astype(ml_dtypes.bfloat16)
    lo = (table - hi.astype(np.float64)).astype(np.float32).astype(ml_dtypes.bfloat16)
    return hi, lo


def make_tables():
    cx, sx = waves(signed(MX))
    cy, sy = waves(signed(MY))
    cz, sz = waves(np.arange(MZ))
    t = {}
    t["zf"] = np.concatenate(halves(np.concatenate([cz, -sz], 0)), 0)
    hi, lo = halves(np.block([[cy.T, -sy.T], [sy.T, cy.T]]))
    t["yf"] = np.concatenate([hi, hi, lo], 0)
    hi, lo = halves(np.concatenate([cx, sx], 0))
    t["xf"] = np.concatenate([hi, lo, hi], 1)
    t["xi"] = np.concatenate([hi.T, lo.T, hi.T], 1)
    hi, lo = halves(np.block([[cy, sy], [-sy, cy]]))
    t["yi"] = np.concatenate([hi, hi, lo], 0)
    hi, lo = halves(np.concatenate([cz, -sz], 0))
    t["zi"] = np.concatenate([hi, hi, lo], 0)
    four = [np.kron(np.eye(4), p.astype(np.float32)).astype(ml_dtypes.bfloat16) for p in (hi, lo)]
    t["zi4"] = np.concatenate([four[0], four[0], four[1]], 0)
    eye = np.eye(C)
    spread_out = np.repeat(eye, C, axis=1)
    spread_in = np.tile(eye, (1, C))
    t["eo"] = np.concatenate([spread_out, spread_out], 0).astype(ml_dtypes.bfloat16)
    t["ei"] = np.concatenate([spread_in, spread_in], 0).astype(ml_dtypes.bfloat16)
    return t


def split(x):
    hi = x.astype(BF)
    lo = (x - hi.astype(F32)).astype(BF)
    return hi, lo


def nn(a, b):
    return lax.dot_general(a, b, (((1,), (0,)), ((), ())), preferred_element_type=F32)


def nt(a, b):
    return lax.dot_general(a, b, (((1,), (1,)), ((), ())), preferred_element_type=F32)


def tn(a, b):
    return lax.dot_general(a, b, (((0,), (0,)), ((), ())), preferred_element_type=F32)


def gelu_slope(h):
    t = jnp.tanh(tanh_scale * (h + cubic_term * h * h * h))
    return 0.5 * (1.0 + t) + 0.5 * h * (1.0 - t * t) * tanh_scale * (1.0 + 3.0 * cubic_term * h * h)


GROUP = 8


def planes_forward(d, first, zf_ref, yf_ref, out2d):
    hi, lo = split(d.reshape(GROUP * N, N))
    a = nt(zf_ref[...], hi)
    z = a[: 2 * MZ] + a[2 * MZ :] + nt(zf_ref[: 2 * MZ, :], lo)
    rows = []
    for c in range(GROUP):
        cols = slice(c * N, (c + 1) * N)
        rows.append(jnp.concatenate([z[:MZ, cols], z[MZ:, cols]], 1))
    hi, lo = split(jnp.concatenate(rows, 0))
    y = nn(jnp.concatenate([hi, lo, hi], 1), yf_ref[...])
    for c in range(GROUP):
        out2d[pl.ds(first + c, MZ, stride=C), :] = y[c * MZ : (c + 1) * MZ, :]


def grad_kernel(pre_ref, cot_ref, zf_ref, yf_ref, gp_ref, out_ref):
    out2d = out_ref.reshape(MZ * C, 2 * MY)
    for g in range(0, C, GROUP):
        gp = cot_ref[0, g : g + GROUP, 0] * gelu_slope(pre_ref[0, g : g + GROUP, 0])
        gp_ref[0, g : g + GROUP, 0] = gp
        planes_forward(gp, g, zf_ref, yf_ref, out2d)


def input_kernel(in_ref, gp_ref, zf_ref, yf_ref, out_ref, acc_ref):
    out2d = out_ref.reshape(MZ * C, 2 * MY)

    @pl.when(pl.program_id(0) == 0)
    def _():
        acc_ref[...] = jnp.zeros_like(acc_ref)

    for g in range(0, C, GROUP):
        planes_forward(in_ref[0, g : g + GROUP, 0], g, zf_ref, yf_ref, out2d)

    def rows(ref, y):
        a = ref[0, :, 0, pl.ds(y, 8), :].reshape(C * 8, N)
        b = ref[0, :, 0, pl.ds(y + 8, 8), :].reshape(C * 8, N)
        return split(jnp.concatenate([a, b], 1))

    @pl.loop(0, N // 16)
    def _(s):
        y = pl.multiple_of(s * 16, 16)
        gh, gl = rows(gp_ref, y)
        ih, il = rows(in_ref, y)
        acc_ref[...] += nt(
            jnp.concatenate([gh, gl, gh], 1), jnp.concatenate([ih, ih, il], 1)
        )


def fold(x):
    total = x[:, :128]
    for t in range(1, C * C // 128):
        total = total + x[:, t * 128 : (t + 1) * 128]
    return total


def swap(x):
    return pltpu.roll(x, MY, 1)


def lane_sign(rows, first):
    lane = lax.broadcasted_iota(jnp.int32, (rows, 2 * MY), 1)
    return jnp.where(lane < MY, first, -first).astype(F32)


def x_forward(a2d, xf_ref):
    for c in range(C):
        hi, lo = split(a2d[pl.ds(c, N, stride=C), :])
        p = nn(xf_ref[...], jnp.concatenate([hi, hi, lo], 0))
        s = (p[:MX] + lane_sign(MX, 1.0) * swap(p[MX:])) * NORM
        yield c, s


def modes_kernel(a_ref, w_ref, xf_ref, xi_ref, eo_ref, s_ref, out_ref, d_ref, *, dp, step):
    mh = MX // dp
    a2d = a_ref.reshape(N * C, 2 * MY)
    s2d = s_ref.reshape(MX * C, 2 * MY)
    out2d = out_ref.reshape(N * C, 2 * MY)
    pid = pl.program_id(0)

    @pl.when(pid == 0)
    def _():
        for c, s in x_forward(a2d, xf_ref):
            for h in range(dp):
                s_ref[h, c] = s[h * mh : (h + 1) * mh]

    for u in range(step):
        m = pid * step + u
        start = (m // mh) * (C * mh) + m % mh
        hi, lo = split(s2d[pl.ds(start, C, stride=mh), :])
        g = tn(jnp.concatenate([hi, lo], 0), eo_ref[...])
        gr, gi = g[:MY], g[MY:]
        wr, wi = w_ref[u, :, : C * C], w_ref[u, :, C * C :]

        both = jnp.concatenate([fold(wr * gr + wi * gi), fold(wr * gi - wi * gr)], 0).T
        total = both[:C] + both[C : 2 * C] + both[2 * C : 3 * C] + both[3 * C :]
        d_ref[pl.ds(m, C, stride=MX), :] = total * NORM

    @pl.when(pid == MX // step - 1)
    def _():
        for i in range(C):
            d = d_ref[i * MX : (i + 1) * MX, :]
            hi, lo = split(jnp.concatenate([d, lane_sign(MX, -1.0) * swap(d)], 0))
            out2d[pl.ds(i, N, stride=C), :] = nn(xi_ref[...], jnp.concatenate([hi, hi, lo], 0))


def spectrum_kernel(a_ref, xf_ref, s_ref, *, dp):
    mh = MX // dp
    a2d = a_ref.reshape(N * C, 2 * MY)
    for c, s in x_forward(a2d, xf_ref):
        for h in range(dp):
            s_ref[h, c] = s[h * mh : (h + 1) * mh]


def weight_kernel(g_ref, i_ref, eo_ref, ei_ref, out_ref, *, dp, step):
    mh = MX // dp
    g2d = g_ref.reshape(MX * C, 2 * MY)
    i2d = i_ref.reshape(MX * C, 2 * MY)
    for u in range(step):
        m = pl.program_id(0) * step + u
        real = imag = None
        for b in range(dp):
            at = pl.ds(b * (C * mh) + m, C, stride=mh)
            g = tn(jnp.concatenate(split(g2d[at, :]), 0), eo_ref[...])
            i = tn(jnp.concatenate(split(i2d[at, :]), 0), ei_ref[...])
            gr, gi, ir, ii = g[:MY], g[MY:], i[:MY], i[MY:]
            r = gr * ir + gi * ii
            j = gi * ir - gr * ii
            real, imag = (r, j) if real is None else (real + r, imag + j)
        out_ref[u, :, : C * C] = real
        out_ref[u, :, C * C :] = imag


def inverse_kernel(b_ref, gp_ref, k_ref, yi_ref, zi_ref, out_ref, re_ref, im_ref):
    hi, lo = split(b_ref.reshape(MZ * C, 2 * MY)[...])
    v = nn(jnp.concatenate([hi, lo, hi], 1), yi_ref[...])
    re_ref[...] = v[:, :N]
    im_ref[...] = v[:, N:]
    for i in range(C):
        at = pl.ds(i, MZ, stride=C)
        hi, lo = split(jnp.concatenate([re_ref[at, :], im_ref[at, :]], 0))
        out_ref[0, i, 0] = tn(jnp.concatenate([hi, lo, hi], 0), zi_ref[...])
    kh, kl = split(k_ref[...])
    k3 = jnp.concatenate([kh, kl, kh], 1)

    @pl.loop(0, N // 16)
    def _(s):
        y = pl.multiple_of(s * 16, 16)
        a = gp_ref[0, :, 0, pl.ds(y, 8), :].reshape(C * 8, N)
        b = gp_ref[0, :, 0, pl.ds(y + 8, 8), :].reshape(C * 8, N)
        gh, gl = split(jnp.concatenate([a, b], 1))
        r = nn(k3, jnp.concatenate([gh, gh, gl], 0))
        out_ref[0, :, 0, pl.ds(y, 8), :] += r[:, :N].reshape(C, 8, N)
        out_ref[0, :, 0, pl.ds(y + 8, 8), :] += r[:, N:].reshape(C, 8, N)


def whole(shape):
    return pl.BlockSpec(shape, lambda *_: (0,) * len(shape))


def params():
    return pltpu.CompilerParams(vmem_limit_bytes=LIMIT)


def cost(flops, nbytes):
    return pl.CostEstimate(flops=int(flops), bytes_accessed=int(nbytes), transcendentals=0)


def body(space, dp, inputs, preact, cotangent, spectral_weight, skip_weight):
    t = {k: jnp.asarray(v) for k, v in make_tables().items()}
    xl = inputs.shape[2]
    kl = spectral_weight.shape[1]
    field = jax.ShapeDtypeStruct(inputs.shape, F32)
    spread = jax.ShapeDtypeStruct((MZ, xl, C, 2 * MY), F32)
    plane = pl.BlockSpec((1, C, 1, N, N), lambda x: (0, 0, x, 0, 0))
    lines = pl.BlockSpec((MZ, 1, C, 2 * MY), lambda x: (0, x, 0, 0))
    nbytes = inputs.size * 4

    gp, part_g = pl.pallas_call(
        grad_kernel,
        grid=(xl,),
        in_specs=[plane, plane, whole(t["zf"].shape), whole(t["yf"].shape)],
        out_specs=[plane, lines],
        out_shape=[field, spread],
        compiler_params=params(),
        cost_estimate=cost(nbytes * 300, nbytes * 4),
        name="grad_forward",
    )(preact, cotangent, t["zf"], t["yf"])
    part_i, acc = pl.pallas_call(
        input_kernel,
        grid=(xl,),
        in_specs=[plane, plane, whole(t["zf"].shape), whole(t["yf"].shape)],
        out_specs=[lines, whole((C * 8, C * 8))],
        out_shape=[spread, jax.ShapeDtypeStruct((C * 8, C * 8), F32)],
        compiler_params=params(),
        cost_estimate=cost(nbytes * 600, nbytes * 3),
        name="input_forward",
    )(inputs, gp, t["zf"], t["yf"])
    diag = jnp.einsum("oyiy->oi", acc.reshape(C, 8, C, 8), precision=lax.Precision.HIGHEST)
    skip_grad = lax.psum(NORM * diag, ("dp", "space"))

    q = space // MZ
    jl = MY // q

    def outward(part):
        p = part.reshape(MZ, xl, C, 2, q, jl).transpose(0, 4, 1, 2, 3, 5)
        p = p.reshape(space, xl, C, 2 * jl)
        return lax.all_to_all(p, "space", split_axis=0, concat_axis=0, tiled=True)

    arrived_g = outward(part_g)
    arrived_i = outward(part_i)
    mh = MX // dp

    if jl == MY and xl == 8:
        step = 4
        spec_shape = (dp, C, mh, 2 * MY)
        spec_g, along = pl.pallas_call(
            functools.partial(modes_kernel, dp=dp, step=step),
            grid=(MX // step,),
            in_specs=[
                whole(arrived_g.shape),
                pl.BlockSpec((step, kl, 2 * C * C), lambda m: (m, 0, 0)),
                whole(t["xf"].shape),
                whole(t["xi"].shape),
                whole(t["eo"].shape),
            ],
            out_specs=[whole(spec_shape), whole(arrived_g.shape)],
            out_shape=[
                jax.ShapeDtypeStruct(spec_shape, F32),
                jax.ShapeDtypeStruct(arrived_g.shape, F32),
            ],
            scratch_shapes=[pltpu.VMEM((C * MX, 2 * MY), F32)],
            compiler_params=params(),
            cost_estimate=cost(1e9, spectral_weight.size * 4 + arrived_g.size * 8),
            name="modes",
        )(arrived_g, spectral_weight, t["xf"], t["xi"], t["eo"])
        spec_i = pl.pallas_call(
            functools.partial(spectrum_kernel, dp=dp),
            in_specs=[whole(arrived_i.shape), whole(t["xf"].shape)],
            out_specs=whole(spec_shape),
            out_shape=jax.ShapeDtypeStruct(spec_shape, F32),
            grid=(1,),
            compiler_params=params(),
            cost_estimate=cost(1e8, arrived_i.size * 5),
            name="spectrum",
        )(arrived_i, t["xf"])
        both_g = lax.all_to_all(spec_g, "dp", split_axis=0, concat_axis=0, tiled=True)
        both_i = lax.all_to_all(spec_i, "dp", split_axis=0, concat_axis=0, tiled=True)
        wstep = 2
        weight_grad = pl.pallas_call(
            functools.partial(weight_kernel, dp=dp, step=wstep),
            grid=(mh // wstep,),
            in_specs=[whole(spec_shape), whole(spec_shape)]
            + [whole(t["eo"].shape), whole(t["ei"].shape)],
            out_specs=pl.BlockSpec((wstep, kl, 2 * C * C), lambda m: (m, 0, 0)),
            out_shape=jax.ShapeDtypeStruct((mh, kl, 2 * C * C), F32),
            compiler_params=params(),
            cost_estimate=cost(1e9, mh * kl * 2 * C * C * 4),
            name="weight_grad",
        )(both_g, both_i, t["eo"], t["ei"])
    else:
        weight_grad, along = modes_plain(space, dp, arrived_g, arrived_i, spectral_weight, jl)

    back = lax.all_to_all(along, "space", split_axis=0, concat_axis=0, tiled=True)
    back = back.reshape(MZ, q, xl, C, 2, jl).transpose(0, 2, 3, 4, 1, 5).reshape(MZ, xl, C, 2 * MY)
    kron = jnp.kron(skip_weight.T, jnp.eye(8, dtype=F32))
    input_grad = pl.pallas_call(
        inverse_kernel,
        grid=(xl,),
        in_specs=[lines, plane, whole(kron.shape), whole(t["yi"].shape), whole(t["zi"].shape)],
        out_specs=plane,
        out_shape=field,
        scratch_shapes=[pltpu.VMEM((MZ * C, N), F32)] * 2,
        compiler_params=params(),
        cost_estimate=cost(nbytes * 600, nbytes * 2),
        name="inverse",
    )(back, gp, kron, t["yi"], t["zi"])
    return input_grad, weight_grad, skip_grad


def modes_plain(space, dp, arrived_g, arrived_i, weights, jl):
    cx, sx = waves(signed(MX))
    fwd = jnp.asarray(np.stack([np.stack([cx.T, -sx.T], 1), np.stack([sx.T, cx.T], 1)], 0), F32)
    inv = jnp.asarray(np.stack([np.stack([cx, sx], 1), np.stack([-sx, cx], 1)], 0), F32)
    ein = functools.partial(jnp.einsum, precision=lax.Precision.HIGHEST)

    def spectrum(a):
        return ein("xcrj,rxsm->scmj", a.reshape(N, C, 2, jl), fwd) * NORM

    g, i = spectrum(arrived_g), spectrum(arrived_i)

    def other(s):
        return lax.all_to_all(s[None], "dp", split_axis=3, concat_axis=0, tiled=True)

    bg, bi = other(g), other(i)
    real = ein("bomk,bimk->mkoi", bg[:, 0], bi[:, 0]) + ein("bomk,bimk->mkoi", bg[:, 1], bi[:, 1])
    imag = ein("bomk,bimk->mkoi", bg[:, 1], bi[:, 0]) - ein("bomk,bimk->mkoi", bg[:, 0], bi[:, 1])
    weight_grad = jnp.stack([real, imag], 2).reshape(MX // dp, jl, 2 * C * C)
    w = weights.reshape(MX, jl, 2, C, C)
    dr = ein("mkoi,omk->imk", w[:, :, 0], g[0]) + ein("mkoi,omk->imk", w[:, :, 1], g[1])
    di = ein("mkoi,omk->imk", w[:, :, 0], g[1]) - ein("mkoi,omk->imk", w[:, :, 1], g[0])
    along = ein("rimk,rmsx->xisk", jnp.stack([dr, di], 0), inv) * NORM
    return weight_grad, along.reshape(arrived_g.shape)


def selector(rows):
    row = lax.broadcasted_iota(jnp.int32, (rows, 8 * C), 0)
    col = lax.broadcasted_iota(jnp.int32, (rows, 8 * C), 1)
    return jnp.where(col // 8 == row, 1.0, 0.0).astype(BF)


def same_row():
    row = lax.broadcasted_iota(jnp.int32, (8 * C, 8 * C), 0)
    col = lax.broadcasted_iota(jnp.int32, (8 * C, 8 * C), 1)
    return row % 8 == col % 8


def fused_kernel(
    pre_ref, cot_ref, in_ref, w_ref, sw_ref, zf_ref, yf_ref, xf_ref, xi_ref, eo_ref,
    skip_ref, mine_ref, theirs_ref, sum_ref, along_ref,
    gp_ref, k_ref, acc_ref, sg_ref, si_ref, spec_ref, rg_ref, ri_ref, d_ref, ss_ref, rs_ref,
    send_g, send_i, send_s, recv_g, recv_i, recv_s,
    *, space, dp, xl, wstep,
):
    step = pl.program_id(0)
    me = lax.axis_index("space")
    half = lax.axis_index("dp")
    mh = MX // dp
    msteps = MX // wstep

    def others(action):
        @pl.loop(1, space)
        def _(r):
            action(lax.rem(me + r, space))

    def put(src, dst, send, recv, target):
        pltpu.make_async_remote_copy(
            src_ref=src, dst_ref=dst, send_sem=send, recv_sem=recv,
            device_id={"space": target}, device_id_type=pl.DeviceIdType.MESH,
        ).start()

    def await_all(ref, sem):
        part = ref.at[pl.ds(0, space - 1)]
        pltpu.make_async_copy(part, part, sem).wait()

    @pl.when(step == 0)
    def _():
        barrier = pltpu.get_barrier_semaphore()

        def greet(target):
            pl.semaphore_signal(
                barrier, inc=1, device_id={"space": target}, device_id_type=pl.DeviceIdType.MESH
            )

        others(greet)
        pl.semaphore_wait(barrier, space - 1)
        acc_ref[...] = jnp.zeros_like(acc_ref)
        sel = selector(C)
        pieces = []
        for piece in split(sw_ref[...]):
            wide = tn(piece, sel).astype(BF)
            pieces.append(jnp.where(same_row(), tn(sel, wide), 0.0).astype(BF))
        k_ref[...] = jnp.concatenate([pieces[0], pieces[1], pieces[0]], 1)

    @pl.when(step < xl)
    def _():
        x = step
        out2d = sg_ref.at[x].reshape(MZ * C, 2 * MY)
        for g in range(0, C, GROUP):
            gp = cot_ref[0, g : g + GROUP, 0] * gelu_slope(pre_ref[0, g : g + GROUP, 0])
            gp_ref[x, g : g + GROUP] = gp
            planes_forward(gp, g, zf_ref, yf_ref, out2d)
        rg_ref[me, x] = sg_ref[x, me]
        others(lambda t: put(sg_ref.at[x, t], rg_ref.at[me, x], send_g, recv_g, t))

    @pl.when((step >= xl) & (step < 2 * xl))
    def _():
        x = step - xl
        out2d = si_ref.at[x].reshape(MZ * C, 2 * MY)
        for g in range(0, C, GROUP):
            planes_forward(in_ref[0, g : g + GROUP, 0], g, zf_ref, yf_ref, out2d)
        ri_ref[me, x] = si_ref[x, me]
        others(lambda t: put(si_ref.at[x, t], ri_ref.at[me, x], send_i, recv_i, t))

        @pl.loop(0, N // 16)
        def _(s):
            y = pl.multiple_of(s * 16, 16)
            ga = gp_ref[x, :, pl.ds(y, 8), :].reshape(C * 8, N)
            gb = gp_ref[x, :, pl.ds(y + 8, 8), :].reshape(C * 8, N)
            gh, gl = split(jnp.concatenate([ga, gb], 1))
            ia = in_ref[0, :, 0, pl.ds(y, 8), :].reshape(C * 8, N)
            ib = in_ref[0, :, 0, pl.ds(y + 8, 8), :].reshape(C * 8, N)
            ih, il = split(jnp.concatenate([ia, ib], 1))
            acc_ref[...] += nt(
                jnp.concatenate([gh, gl, gh], 1), jnp.concatenate([ih, ih, il], 1)
            )
            r = nn(k_ref[...], jnp.concatenate([gh, gh, gl], 0))
            skip_ref[0, :, 0, pl.ds(y, 8), :] = r[:, :N].reshape(C, 8, N)
            skip_ref[0, :, 0, pl.ds(y + 8, 8), :] = r[:, N:].reshape(C, 8, N)

    @pl.when(step == 2 * xl - 1)
    def _():
        hi, lo = split(jnp.where(same_row(), acc_ref[...], 0.0))
        sel = selector(C)
        hi, lo = split(nn(sel, hi) + nn(sel, lo))
        wide = selector(128)
        ss_ref[...] = nt(hi, wide) + nt(lo, wide)
        rs_ref[me] = ss_ref[...]
        others(lambda t: put(ss_ref, rs_ref.at[me], send_s, recv_s, t))

    s2d = spec_ref.reshape(dp * 2 * C * mh, 2 * MY)

    @pl.when(step == 2 * xl)
    def _():
        await_all(rg_ref, recv_g)
        await_all(rg_ref, send_g)
        for c, s in x_forward(rg_ref.reshape(N * C, 2 * MY), xf_ref):
            for h in range(dp):
                spec_ref[lax.rem(h + half, dp), 0, c] = s[h * mh : (h + 1) * mh]

    @pl.when(step >= 2 * xl)
    def _():
        for u in range(wstep):
            m = (step - 2 * xl) * wstep + u
            slot = lax.rem(m // mh + half, dp)
            start = slot * (2 * C * mh) + lax.rem(m, mh)
            hi, lo = split(s2d[pl.ds(start, C, stride=mh), :])
            g = tn(jnp.concatenate([hi, lo], 0), eo_ref[...])
            gr, gi = g[:MY], g[MY:]
            wr, wi = w_ref[u, :, : C * C], w_ref[u, :, C * C :]
            both = jnp.concatenate([fold(wr * gr + wi * gi), fold(wr * gi - wi * gr)], 0).T
            total = both[:C] + both[C : 2 * C] + both[2 * C : 3 * C] + both[3 * C :]
            d_ref[pl.ds(m, C, stride=MX), :] = total * NORM

    @pl.when(step == 2 * xl + msteps - 1)
    def _():
        out2d = along_ref.reshape(N * C, 2 * MY)
        for i in range(C):
            d = d_ref[i * MX : (i + 1) * MX, :]
            hi, lo = split(jnp.concatenate([d, lane_sign(MX, -1.0) * swap(d)], 0))
            out2d[pl.ds(i, N, stride=C), :] = nn(xi_ref[...], jnp.concatenate([hi, hi, lo], 0))
        await_all(rs_ref, recv_s)
        await_all(rs_ref, send_s)
        total = rs_ref[0]
        for r in range(1, space):
            total = total + rs_ref[r]
        sum_ref[...] = total
        await_all(ri_ref, recv_i)
        await_all(ri_ref, send_i)
        for c, s in x_forward(ri_ref.reshape(N * C, 2 * MY), xf_ref):
            for h in range(dp):
                spec_ref[lax.rem(h + half, dp), 1, c] = s[h * mh : (h + 1) * mh]
        mine_ref[...] = spec_ref[0]
        theirs_ref[...] = spec_ref[1]


def pair_weight_kernel(mine_ref, other_ref, eo_ref, ei_ref, out_ref, *, step):
    mh = mine_ref.shape[2]
    rows = 2 * C * mh
    half = rows // 2
    for u in range(step):
        m = pl.program_id(0) * step + u
        real = imag = None
        for ref in (mine_ref, other_ref):
            flat = ref.reshape(rows, 2 * MY)
            gs = flat[pl.ds(m, C, stride=mh), :]
            vs = flat[pl.ds(half + m, C, stride=mh), :]
            g = tn(jnp.concatenate(split(gs), 0), eo_ref[...])
            i = tn(jnp.concatenate(split(vs), 0), ei_ref[...])
            gr, gi, ir, ii = g[:MY], g[MY:], i[:MY], i[MY:]
            r = gr * ir + gi * ii
            j = gi * ir - gr * ii
            real, imag = (r, j) if real is None else (real + r, imag + j)
        out_ref[u, :, : C * C] = real
        out_ref[u, :, C * C :] = imag


def restore_kernel(b_ref, sk_ref, yi_ref, zi_ref, out_ref, re_ref, im_ref):
    hi, lo = split(b_ref.reshape(MZ * C, 2 * MY)[...])
    v = nn(jnp.concatenate([hi, lo, hi], 1), yi_ref[...])
    re_ref[...] = v[:, :N]
    im_ref[...] = v[:, N:]
    for first in range(0, C, 16):
        turned = []
        for q in range(first, first + 16, 4):
            pieces = []
            for i in range(q, q + 4):
                at = pl.ds(i, MZ, stride=C)
                pieces += [re_ref[at, :], im_ref[at, :]]
            turned.append(jnp.concatenate(pieces, 0).T)
        hi, lo = split(jnp.concatenate(turned, 0))
        r = nn(jnp.concatenate([hi, lo, hi], 1), zi_ref[...])
        for k in range(16):
            rows = slice(k // 4 * N, (k // 4 + 1) * N)
            cols = slice(k % 4 * N, (k % 4 + 1) * N)
            out_ref[0, first + k, 0] = sk_ref[0, first + k, 0] + r[rows, cols]


def fused_body(space, dp, inputs, preact, cotangent, spectral_weight, skip_weight):
    t = {k: jnp.asarray(v) for k, v in make_tables().items()}
    xl = inputs.shape[2]
    kl = spectral_weight.shape[1]
    mh = MX // dp
    field = jax.ShapeDtypeStruct(inputs.shape, F32)
    wstep = 4
    last = MX // wstep - 1
    nbytes = inputs.size * 4

    def plane(first):
        return pl.BlockSpec((1, C, 1, N, N), lambda s: (0, 0, jnp.clip(s - first, 0, xl - 1), 0, 0))

    arrive = (space, xl, C, 2 * MY)
    send = (xl, space, C, 2 * MY)
    half_shape = (2, C, mh, 2 * MY)
    spec_shape = (dp,) + half_shape
    dma = pltpu.SemaphoreType.DMA
    skip_term, mine, send_half, summed, along = pl.pallas_call(
        functools.partial(fused_kernel, space=space, dp=dp, xl=xl, wstep=wstep),
        grid=(2 * xl + MX // wstep,),
        in_specs=[
            plane(0),
            plane(0),
            plane(xl),
            pl.BlockSpec(
                (wstep, kl, 2 * C * C), lambda s: (jnp.clip(s - 2 * xl, 0, last), 0, 0)
            ),
            whole(skip_weight.shape),
            whole(t["zf"].shape),
            whole(t["yf"].shape),
            whole(t["xf"].shape),
            whole(t["xi"].shape),
            whole(t["eo"].shape),
        ],
        out_specs=[
            plane(xl),
            whole(half_shape),
            whole(half_shape),
            whole((C, 128)),
            whole(arrive),
        ],
        out_shape=[
            field,
            jax.ShapeDtypeStruct(half_shape, F32),
            jax.ShapeDtypeStruct(half_shape, F32),
            jax.ShapeDtypeStruct((C, 128), F32),
            jax.ShapeDtypeStruct(arrive, F32),
        ],
        scratch_shapes=[
            pltpu.VMEM((xl, C, N, N), F32),
            pltpu.VMEM((8 * C, 24 * C), BF),
            pltpu.VMEM((8 * C, 8 * C), F32),
            pltpu.VMEM(send, F32),
            pltpu.VMEM(send, F32),
            pltpu.VMEM(spec_shape, F32),
            pltpu.VMEM(arrive, F32),
            pltpu.VMEM(arrive, F32),
            pltpu.VMEM((C * MX, 2 * MY), F32),
            pltpu.VMEM((C, 128), F32),
            pltpu.VMEM((space, C, 128), F32),
        ]
        + [dma] * 6,
        compiler_params=pltpu.CompilerParams(
            vmem_limit_bytes=FUSED_LIMIT, collective_id=0, has_side_effects=True
        ),
        cost_estimate=cost(nbytes * 1500, nbytes * 5),
        name="fused_forward",
    )(
        preact, cotangent, inputs, spectral_weight, skip_weight,
        t["zf"], t["yf"], t["xf"], t["xi"], t["eo"],
    )
    pairs = [(0, 1), (1, 0)]
    back = lax.all_to_all(along, "space", split_axis=0, concat_axis=0, tiled=True)
    theirs = lax.ppermute(send_half, "dp", pairs)
    skip_grad = NORM * (summed + lax.ppermute(summed, "dp", pairs))[:, :C]
    input_grad = pl.pallas_call(
        restore_kernel,
        grid=(xl,),
        in_specs=[
            pl.BlockSpec((MZ, 1, C, 2 * MY), lambda x: (0, x, 0, 0)),
            pl.BlockSpec((1, C, 1, N, N), lambda x: (0, 0, x, 0, 0)),
            whole(t["yi"].shape),
            whole(t["zi4"].shape),
        ],
        out_specs=pl.BlockSpec((1, C, 1, N, N), lambda x: (0, 0, x, 0, 0)),
        out_shape=field,
        scratch_shapes=[pltpu.VMEM((MZ * C, N), F32)] * 2,
        compiler_params=params(),
        cost_estimate=cost(nbytes * 300, nbytes * 2),
        name="inverse",
    )(back, skip_term, t["yi"], t["zi4"])
    step = 2
    weight_grad = pl.pallas_call(
        functools.partial(pair_weight_kernel, step=step),
        grid=(mh // step,),
        in_specs=[
            whole(half_shape),
            whole(half_shape),
            whole(t["eo"].shape),
            whole(t["ei"].shape),
        ],
        out_specs=pl.BlockSpec((step, kl, 2 * C * C), lambda m: (m, 0, 0)),
        out_shape=jax.ShapeDtypeStruct((mh, kl, 2 * C * C), F32),
        compiler_params=params(),
        cost_estimate=cost(1e9, mh * kl * 2 * C * C * 4),
        name="weight_grad",
    )(mine, theirs, t["eo"], t["ei"])
    return input_grad, weight_grad, skip_grad


def solution(mesh):
    in_specs = (
        P("dp", None, "space", None, None),
        P("dp", None, "space", None, None),
        P("dp", None, "space", None, None),
        P(None, "space", None),
        P(),
    )
    out_specs = (P("dp", None, "space", None, None), P("dp", "space", None), P())
    space, dp = mesh.shape["space"], mesh.shape["dp"]
    form = fused_body if space == MZ and dp == 2 else body
    local = functools.partial(form, space, dp)
    return jax.shard_map(local, mesh=mesh, in_specs=in_specs, out_specs=out_specs, check_vma=False)
```

```python
import functools

import jax
import jax.numpy as jnp
import ml_dtypes
import numpy as np
from jax import lax
from jax.experimental import pallas as pl
from jax.experimental.pallas import tpu as pltpu
from jax.sharding import PartitionSpec as P

N = 128
C = 32
MX = 32
MY = 64
MZ = 16
NORM = float(N) ** -1.5

tanh_scale = 0.7978845608028654
cubic_term = 0.044715
BF = jnp.bfloat16
F32 = jnp.float32
LIMIT = 48 * 1024 * 1024
FUSED_LIMIT = 60 * 1024 * 1024


def signed(count):
    p = np.arange(count)
    return np.where(p < count // 2, p, p - count)


def waves(freq):
    angle = 2 * np.pi / N * np.mod(freq[:, None] * np.arange(N)[None, :], N)
    return np.cos(angle), np.sin(angle)


def halves(table):
    hi = table.astype(np.float32).astype(ml_dtypes.bfloat16)
    lo = (table - hi.astype(np.float64)).astype(np.float32).astype(ml_dtypes.bfloat16)
    return hi, lo


def make_tables():
    cx, sx = waves(signed(MX))
    cy, sy = waves(signed(MY))
    cz, sz = waves(np.arange(MZ))
    t = {}
    t["zf"] = np.concatenate(halves(np.concatenate([cz, -sz], 0)), 0)
    hi, lo = halves(np.block([[cy.T, -sy.T], [sy.T, cy.T]]))
    t["yf"] = np.concatenate([hi, hi, lo], 0)
    hi, lo = halves(np.concatenate([cx, sx], 0))
    t["xf"] = np.concatenate([hi, lo, hi], 1)
    t["xi"] = np.concatenate([hi.T, lo.T, hi.T], 1)
    hi, lo = halves(np.block([[cy, sy], [-sy, cy]]))
    t["yi"] = np.concatenate([hi, hi, lo], 0)
    hi, lo = halves(np.concatenate([cz, -sz], 0))
    t["zi"] = np.concatenate([hi, hi, lo], 0)
    four = [np.kron(np.eye(4), p.astype(np.float32)).astype(ml_dtypes.bfloat16) for p in (hi, lo)]
    t["zi4"] = np.concatenate([four[0], four[0], four[1]], 0)
    eye = np.eye(C)
    spread_out = np.repeat(eye, C, axis=1)
    spread_in = np.tile(eye, (1, C))
    t["eo"] = np.concatenate([spread_out, spread_out], 0).astype(ml_dtypes.bfloat16)
    t["ei"] = np.concatenate([spread_in, spread_in], 0).astype(ml_dtypes.bfloat16)
    return t


def split(x):
    hi = x.astype(BF)
    lo = (x - hi.astype(F32)).astype(BF)
    return hi, lo


def nn(a, b):
    return lax.dot_general(a, b, (((1,), (0,)), ((), ())), preferred_element_type=F32)


def nt(a, b):
    return lax.dot_general(a, b, (((1,), (1,)), ((), ())), preferred_element_type=F32)


def tn(a, b):
    return lax.dot_general(a, b, (((0,), (0,)), ((), ())), preferred_element_type=F32)


def gelu_slope(h):
    t = jnp.tanh(tanh_scale * (h + cubic_term * h * h * h))
    return 0.5 * (1.0 + t) + 0.5 * h * (1.0 - t * t) * tanh_scale * (1.0 + 3.0 * cubic_term * h * h)


GROUP = 8


def planes_forward(d, first, zf_ref, yf_ref, out2d):
    hi, lo = split(d.reshape(GROUP * N, N))
    a = nt(zf_ref[...], hi)
    z = a[: 2 * MZ] + a[2 * MZ :] + nt(zf_ref[: 2 * MZ, :], lo)
    rows = []
    for c in range(GROUP):
        cols = slice(c * N, (c + 1) * N)
        rows.append(jnp.concatenate([z[:MZ, cols], z[MZ:, cols]], 1))
    hi, lo = split(jnp.concatenate(rows, 0))
    y = nn(jnp.concatenate([hi, lo, hi], 1), yf_ref[...])
    for c in range(GROUP):
        out2d[pl.ds(first + c, MZ, stride=C), :] = y[c * MZ : (c + 1) * MZ, :]


def grad_kernel(pre_ref, cot_ref, zf_ref, yf_ref, gp_ref, out_ref):
    out2d = out_ref.reshape(MZ * C, 2 * MY)
    for g in range(0, C, GROUP):
        gp = cot_ref[0, g : g + GROUP, 0] * gelu_slope(pre_ref[0, g : g + GROUP, 0])
        gp_ref[0, g : g + GROUP, 0] = gp
        planes_forward(gp, g, zf_ref, yf_ref, out2d)


def input_kernel(in_ref, gp_ref, zf_ref, yf_ref, out_ref, acc_ref):
    out2d = out_ref.reshape(MZ * C, 2 * MY)

    @pl.when(pl.program_id(0) == 0)
    def _():
        acc_ref[...] = jnp.zeros_like(acc_ref)

    for g in range(0, C, GROUP):
        planes_forward(in_ref[0, g : g + GROUP, 0], g, zf_ref, yf_ref, out2d)

    def rows(ref, y):
        a = ref[0, :, 0, pl.ds(y, 8), :].reshape(C * 8, N)
        b = ref[0, :, 0, pl.ds(y + 8, 8), :].reshape(C * 8, N)
        return split(jnp.concatenate([a, b], 1))

    @pl.loop(0, N // 16)
    def _(s):
        y = pl.multiple_of(s * 16, 16)
        gh, gl = rows(gp_ref, y)
        ih, il = rows(in_ref, y)
        acc_ref[...] += nt(
            jnp.concatenate([gh, gl, gh], 1), jnp.concatenate([ih, ih, il], 1)
        )


def fold(x):
    total = x[:, :128]
    for t in range(1, C * C // 128):
        total = total + x[:, t * 128 : (t + 1) * 128]
    return total


def swap(x):
    return pltpu.roll(x, MY, 1)


def lane_sign(rows, first):
    lane = lax.broadcasted_iota(jnp.int32, (rows, 2 * MY), 1)
    return jnp.where(lane < MY, first, -first).astype(F32)


def x_forward(a2d, xf_ref):
    for c in range(C):
        hi, lo = split(a2d[pl.ds(c, N, stride=C), :])
        p = nn(xf_ref[...], jnp.concatenate([hi, hi, lo], 0))
        s = (p[:MX] + lane_sign(MX, 1.0) * swap(p[MX:])) * NORM
        yield c, s


def modes_kernel(a_ref, w_ref, xf_ref, xi_ref, eo_ref, s_ref, out_ref, d_ref, *, dp, step):
    mh = MX // dp
    a2d = a_ref.reshape(N * C, 2 * MY)
    s2d = s_ref.reshape(MX * C, 2 * MY)
    out2d = out_ref.reshape(N * C, 2 * MY)
    pid = pl.program_id(0)

    @pl.when(pid == 0)
    def _():
        for c, s in x_forward(a2d, xf_ref):
            for h in range(dp):
                s_ref[h, c] = s[h * mh : (h + 1) * mh]

    for u in range(step):
        m = pid * step + u
        start = (m // mh) * (C * mh) + m % mh
        hi, lo = split(s2d[pl.ds(start, C, stride=mh), :])
        g = tn(jnp.concatenate([hi, lo], 0), eo_ref[...])
        gr, gi = g[:MY], g[MY:]
        wr, wi = w_ref[u, :, : C * C], w_ref[u, :, C * C :]

        both = jnp.concatenate([fold(wr * gr + wi * gi), fold(wr * gi - wi * gr)], 0).T
        total = both[:C] + both[C : 2 * C] + both[2 * C : 3 * C] + both[3 * C :]
        d_ref[pl.ds(m, C, stride=MX), :] = total * NORM

    @pl.when(pid == MX // step - 1)
    def _():
        for i in range(C):
            d = d_ref[i * MX : (i + 1) * MX, :]
            hi, lo = split(jnp.concatenate([d, lane_sign(MX, -1.0) * swap(d)], 0))
            out2d[pl.ds(i, N, stride=C), :] = nn(xi_ref[...], jnp.concatenate([hi, hi, lo], 0))


def spectrum_kernel(a_ref, xf_ref, s_ref, *, dp):
    mh = MX // dp
    a2d = a_ref.reshape(N * C, 2 * MY)
    for c, s in x_forward(a2d, xf_ref):
        for h in range(dp):
            s_ref[h, c] = s[h * mh : (h + 1) * mh]


def weight_kernel(g_ref, i_ref, eo_ref, ei_ref, out_ref, *, dp, step):
    mh = MX // dp
    g2d = g_ref.reshape(MX * C, 2 * MY)
    i2d = i_ref.reshape(MX * C, 2 * MY)
    for u in range(step):
        m = pl.program_id(0) * step + u
        real = imag = None
        for b in range(dp):
            at = pl.ds(b * (C * mh) + m, C, stride=mh)
            g = tn(jnp.concatenate(split(g2d[at, :]), 0), eo_ref[...])
            i = tn(jnp.concatenate(split(i2d[at, :]), 0), ei_ref[...])
            gr, gi, ir, ii = g[:MY], g[MY:], i[:MY], i[MY:]
            r = gr * ir + gi * ii
            j = gi * ir - gr * ii
            real, imag = (r, j) if real is None else (real + r, imag + j)
        out_ref[u, :, : C * C] = real
        out_ref[u, :, C * C :] = imag


def inverse_kernel(b_ref, gp_ref, k_ref, yi_ref, zi_ref, out_ref, re_ref, im_ref):
    hi, lo = split(b_ref.reshape(MZ * C, 2 * MY)[...])
    v = nn(jnp.concatenate([hi, lo, hi], 1), yi_ref[...])
    re_ref[...] = v[:, :N]
    im_ref[...] = v[:, N:]
    for i in range(C):
        at = pl.ds(i, MZ, stride=C)
        hi, lo = split(jnp.concatenate([re_ref[at, :], im_ref[at, :]], 0))
        out_ref[0, i, 0] = tn(jnp.concatenate([hi, lo, hi], 0), zi_ref[...])
    kh, kl = split(k_ref[...])
    k3 = jnp.concatenate([kh, kl, kh], 1)

    @pl.loop(0, N // 16)
    def _(s):
        y = pl.multiple_of(s * 16, 16)
        a = gp_ref[0, :, 0, pl.ds(y, 8), :].reshape(C * 8, N)
        b = gp_ref[0, :, 0, pl.ds(y + 8, 8), :].reshape(C * 8, N)
        gh, gl = split(jnp.concatenate([a, b], 1))
        r = nn(k3, jnp.concatenate([gh, gh, gl], 0))
        out_ref[0, :, 0, pl.ds(y, 8), :] += r[:, :N].reshape(C, 8, N)
        out_ref[0, :, 0, pl.ds(y + 8, 8), :] += r[:, N:].reshape(C, 8, N)


def whole(shape):
    return pl.BlockSpec(shape, lambda *_: (0,) * len(shape))


def params():
    return pltpu.CompilerParams(vmem_limit_bytes=LIMIT)


def cost(flops, nbytes):
    return pl.CostEstimate(flops=int(flops), bytes_accessed=int(nbytes), transcendentals=0)


def body(space, dp, inputs, preact, cotangent, spectral_weight, skip_weight):
    t = {k: jnp.asarray(v) for k, v in make_tables().items()}
    xl = inputs.shape[2]
    kl = spectral_weight.shape[1]
    field = jax.ShapeDtypeStruct(inputs.shape, F32)
    spread = jax.ShapeDtypeStruct((MZ, xl, C, 2 * MY), F32)
    plane = pl.BlockSpec((1, C, 1, N, N), lambda x: (0, 0, x, 0, 0))
    lines = pl.BlockSpec((MZ, 1, C, 2 * MY), lambda x: (0, x, 0, 0))
    nbytes = inputs.size * 4

    gp, part_g = pl.pallas_call(
        grad_kernel,
        grid=(xl,),
        in_specs=[plane, plane, whole(t["zf"].shape), whole(t["yf"].shape)],
        out_specs=[plane, lines],
        out_shape=[field, spread],
        compiler_params=params(),
        cost_estimate=cost(nbytes * 300, nbytes * 4),
        name="grad_forward",
    )(preact, cotangent, t["zf"], t["yf"])
    part_i, acc = pl.pallas_call(
        input_kernel,
        grid=(xl,),
        in_specs=[plane, plane, whole(t["zf"].shape), whole(t["yf"].shape)],
        out_specs=[lines, whole((C * 8, C * 8))],
        out_shape=[spread, jax.ShapeDtypeStruct((C * 8, C * 8), F32)],
        compiler_params=params(),
        cost_estimate=cost(nbytes * 600, nbytes * 3),
        name="input_forward",
    )(inputs, gp, t["zf"], t["yf"])
    diag = jnp.einsum("oyiy->oi", acc.reshape(C, 8, C, 8), precision=lax.Precision.HIGHEST)
    skip_grad = lax.psum(NORM * diag, ("dp", "space"))

    q = space // MZ
    jl = MY // q

    def outward(part):
        p = part.reshape(MZ, xl, C, 2, q, jl).transpose(0, 4, 1, 2, 3, 5)
        p = p.reshape(space, xl, C, 2 * jl)
        return lax.all_to_all(p, "space", split_axis=0, concat_axis=0, tiled=True)

    arrived_g = outward(part_g)
    arrived_i = outward(part_i)
    mh = MX // dp

    if jl == MY and xl == 8:
        step = 4
        spec_shape = (dp, C, mh, 2 * MY)
        spec_g, along = pl.pallas_call(
            functools.partial(modes_kernel, dp=dp, step=step),
            grid=(MX // step,),
            in_specs=[
                whole(arrived_g.shape),
                pl.BlockSpec((step, kl, 2 * C * C), lambda m: (m, 0, 0)),
                whole(t["xf"].shape),
                whole(t["xi"].shape),
                whole(t["eo"].shape),
            ],
            out_specs=[whole(spec_shape), whole(arrived_g.shape)],
            out_shape=[
                jax.ShapeDtypeStruct(spec_shape, F32),
                jax.ShapeDtypeStruct(arrived_g.shape, F32),
            ],
            scratch_shapes=[pltpu.VMEM((C * MX, 2 * MY), F32)],
            compiler_params=params(),
            cost_estimate=cost(1e9, spectral_weight.size * 4 + arrived_g.size * 8),
            name="modes",
        )(arrived_g, spectral_weight, t["xf"], t["xi"], t["eo"])
        spec_i = pl.pallas_call(
            functools.partial(spectrum_kernel, dp=dp),
            in_specs=[whole(arrived_i.shape), whole(t["xf"].shape)],
            out_specs=whole(spec_shape),
            out_shape=jax.ShapeDtypeStruct(spec_shape, F32),
            grid=(1,),
            compiler_params=params(),
            cost_estimate=cost(1e8, arrived_i.size * 5),
            name="spectrum",
        )(arrived_i, t["xf"])
        both_g = lax.all_to_all(spec_g, "dp", split_axis=0, concat_axis=0, tiled=True)
        both_i = lax.all_to_all(spec_i, "dp", split_axis=0, concat_axis=0, tiled=True)
        wstep = 2
        weight_grad = pl.pallas_call(
            functools.partial(weight_kernel, dp=dp, step=wstep),
            grid=(mh // wstep,),
            in_specs=[whole(spec_shape), whole(spec_shape)]
            + [whole(t["eo"].shape), whole(t["ei"].shape)],
            out_specs=pl.BlockSpec((wstep, kl, 2 * C * C), lambda m: (m, 0, 0)),
            out_shape=jax.ShapeDtypeStruct((mh, kl, 2 * C * C), F32),
            compiler_params=params(),
            cost_estimate=cost(1e9, mh * kl * 2 * C * C * 4),
            name="weight_grad",
        )(both_g, both_i, t["eo"], t["ei"])
    else:
        weight_grad, along = modes_plain(space, dp, arrived_g, arrived_i, spectral_weight, jl)

    back = lax.all_to_all(along, "space", split_axis=0, concat_axis=0, tiled=True)
    back = back.reshape(MZ, q, xl, C, 2, jl).transpose(0, 2, 3, 4, 1, 5).reshape(MZ, xl, C, 2 * MY)
    kron = jnp.kron(skip_weight.T, jnp.eye(8, dtype=F32))
    input_grad = pl.pallas_call(
        inverse_kernel,
        grid=(xl,),
        in_specs=[lines, plane, whole(kron.shape), whole(t["yi"].shape), whole(t["zi"].shape)],
        out_specs=plane,
        out_shape=field,
        scratch_shapes=[pltpu.VMEM((MZ * C, N), F32)] * 2,
        compiler_params=params(),
        cost_estimate=cost(nbytes * 600, nbytes * 2),
        name="inverse",
    )(back, gp, kron, t["yi"], t["zi"])
    return input_grad, weight_grad, skip_grad


def modes_plain(space, dp, arrived_g, arrived_i, weights, jl):
    cx, sx = waves(signed(MX))
    fwd = jnp.asarray(np.stack([np.stack([cx.T, -sx.T], 1), np.stack([sx.T, cx.T], 1)], 0), F32)
    inv = jnp.asarray(np.stack([np.stack([cx, sx], 1), np.stack([-sx, cx], 1)], 0), F32)
    ein = functools.partial(jnp.einsum, precision=lax.Precision.HIGHEST)

    def spectrum(a):
        return ein("xcrj,rxsm->scmj", a.reshape(N, C, 2, jl), fwd) * NORM

    g, i = spectrum(arrived_g), spectrum(arrived_i)

    def other(s):
        return lax.all_to_all(s[None], "dp", split_axis=3, concat_axis=0, tiled=True)

    bg, bi = other(g), other(i)
    real = ein("bomk,bimk->mkoi", bg[:, 0], bi[:, 0]) + ein("bomk,bimk->mkoi", bg[:, 1], bi[:, 1])
    imag = ein("bomk,bimk->mkoi", bg[:, 1], bi[:, 0]) - ein("bomk,bimk->mkoi", bg[:, 0], bi[:, 1])
    weight_grad = jnp.stack([real, imag], 2).reshape(MX // dp, jl, 2 * C * C)
    w = weights.reshape(MX, jl, 2, C, C)
    dr = ein("mkoi,omk->imk", w[:, :, 0], g[0]) + ein("mkoi,omk->imk", w[:, :, 1], g[1])
    di = ein("mkoi,omk->imk", w[:, :, 0], g[1]) - ein("mkoi,omk->imk", w[:, :, 1], g[0])
    along = ein("rimk,rmsx->xisk", jnp.stack([dr, di], 0), inv) * NORM
    return weight_grad, along.reshape(arrived_g.shape)


def selector(rows):
    row = lax.broadcasted_iota(jnp.int32, (rows, 8 * C), 0)
    col = lax.broadcasted_iota(jnp.int32, (rows, 8 * C), 1)
    return jnp.where(col // 8 == row, 1.0, 0.0).astype(BF)


def same_row():
    row = lax.broadcasted_iota(jnp.int32, (8 * C, 8 * C), 0)
    col = lax.broadcasted_iota(jnp.int32, (8 * C, 8 * C), 1)
    return row % 8 == col % 8


def fused_kernel(
    pre_ref, cot_ref, in_ref, w_ref, sw_ref, zf_ref, yf_ref, xf_ref, xi_ref, eo_ref,
    skip_ref, mine_ref, theirs_ref, sum_ref, back_ref,
    gp_ref, k_ref, acc_ref, sg_ref, si_ref, sb_ref, spec_ref, rg_ref, ri_ref, d_ref, ss_ref, rs_ref,
    send_g, send_i, send_b, send_s, recv_g, recv_i, recv_b, recv_s, local,
    *, space, dp, xl, wstep,
):
    step = pl.program_id(0)
    me = lax.axis_index("space")
    half = lax.axis_index("dp")
    mh = MX // dp
    msteps = MX // wstep

    def others(action):
        @pl.loop(1, space)
        def _(r):
            action(lax.rem(me + r, space))

    def put(src, dst, send, recv, target):
        pltpu.make_async_remote_copy(
            src_ref=src, dst_ref=dst, send_sem=send, recv_sem=recv,
            device_id={"space": target}, device_id_type=pl.DeviceIdType.MESH,
        ).start()

    def await_all(ref, sem):
        part = ref.at[pl.ds(0, space - 1)]
        pltpu.make_async_copy(part, part, sem).wait()

    @pl.when(step == 0)
    def _():
        barrier = pltpu.get_barrier_semaphore()

        def greet(target):
            pl.semaphore_signal(
                barrier, inc=1, device_id={"space": target}, device_id_type=pl.DeviceIdType.MESH
            )

        others(greet)
        pl.semaphore_wait(barrier, space - 1)
        acc_ref[...] = jnp.zeros_like(acc_ref)
        sel = selector(C)
        pieces = []
        for piece in split(sw_ref[...]):
            wide = tn(piece, sel).astype(BF)
            pieces.append(jnp.where(same_row(), tn(sel, wide), 0.0).astype(BF))
        k_ref[...] = jnp.concatenate([pieces[0], pieces[1], pieces[0]], 1)

    @pl.when(step < xl)
    def _():
        x = step
        out2d = sg_ref.at[x].reshape(MZ * C, 2 * MY)
        for g in range(0, C, GROUP):
            gp = cot_ref[0, g : g + GROUP, 0] * gelu_slope(pre_ref[0, g : g + GROUP, 0])
            gp_ref[x, g : g + GROUP] = gp
            planes_forward(gp, g, zf_ref, yf_ref, out2d)
        rg_ref[me, x] = sg_ref[x, me]
        others(lambda t: put(sg_ref.at[x, t], rg_ref.at[me, x], send_g, recv_g, t))

    @pl.when((step >= xl) & (step < 2 * xl))
    def _():
        x = step - xl
        out2d = si_ref.at[x].reshape(MZ * C, 2 * MY)
        for g in range(0, C, GROUP):
            planes_forward(in_ref[0, g : g + GROUP, 0], g, zf_ref, yf_ref, out2d)
        ri_ref[me, x] = si_ref[x, me]
        others(lambda t: put(si_ref.at[x, t], ri_ref.at[me, x], send_i, recv_i, t))

    @pl.when(step >= 2 * xl + msteps)
    def _():
        x = step - 2 * xl - msteps

        @pl.loop(0, N // 16)
        def _(s):
            y = pl.multiple_of(s * 16, 16)
            ga = gp_ref[x, :, pl.ds(y, 8), :].reshape(C * 8, N)
            gb = gp_ref[x, :, pl.ds(y + 8, 8), :].reshape(C * 8, N)
            gh, gl = split(jnp.concatenate([ga, gb], 1))
            ia = in_ref[0, :, 0, pl.ds(y, 8), :].reshape(C * 8, N)
            ib = in_ref[0, :, 0, pl.ds(y + 8, 8), :].reshape(C * 8, N)
            ih, il = split(jnp.concatenate([ia, ib], 1))
            acc_ref[...] += nt(
                jnp.concatenate([gh, gl, gh], 1), jnp.concatenate([ih, ih, il], 1)
            )
            r = nn(k_ref[...], jnp.concatenate([gh, gh, gl], 0))
            skip_ref[0, :, 0, pl.ds(y, 8), :] = r[:, :N].reshape(C, 8, N)
            skip_ref[0, :, 0, pl.ds(y + 8, 8), :] = r[:, N:].reshape(C, 8, N)

    @pl.when(step == 3 * xl + msteps - 1)
    def _():
        hi, lo = split(jnp.where(same_row(), acc_ref[...], 0.0))
        sel = selector(C)
        hi, lo = split(nn(sel, hi) + nn(sel, lo))
        wide = selector(128)
        ss_ref[...] = nt(hi, wide) + nt(lo, wide)
        rs_ref[me] = ss_ref[...]
        others(lambda t: put(ss_ref, rs_ref.at[me], send_s, recv_s, t))

    s2d = spec_ref.reshape(dp * 2 * C * mh, 2 * MY)

    @pl.when(step == 2 * xl)
    def _():
        await_all(rg_ref, recv_g)
        await_all(rg_ref, send_g)
        for c, s in x_forward(rg_ref.reshape(N * C, 2 * MY), xf_ref):
            for h in range(dp):
                spec_ref[lax.rem(h + half, dp), 0, c] = s[h * mh : (h + 1) * mh]

    @pl.when((step >= 2 * xl) & (step < 2 * xl + msteps))
    def _():
        for u in range(wstep):
            m = (step - 2 * xl) * wstep + u
            slot = lax.rem(m // mh + half, dp)
            start = slot * (2 * C * mh) + lax.rem(m, mh)
            hi, lo = split(s2d[pl.ds(start, C, stride=mh), :])
            g = tn(jnp.concatenate([hi, lo], 0), eo_ref[...])
            gr, gi = g[:MY], g[MY:]
            wr, wi = w_ref[u, :, : C * C], w_ref[u, :, C * C :]
            both = jnp.concatenate([fold(wr * gr + wi * gi), fold(wr * gi - wi * gr)], 0).T
            total = both[:C] + both[C : 2 * C] + both[2 * C : 3 * C] + both[3 * C :]
            d_ref[pl.ds(m, C, stride=MX), :] = total * NORM

    @pl.when(step == 2 * xl + msteps - 1)
    def _():
        out2d = sb_ref.reshape(N * C, 2 * MY)
        for i in range(C):
            d = d_ref[i * MX : (i + 1) * MX, :]
            hi, lo = split(jnp.concatenate([d, lane_sign(MX, -1.0) * swap(d)], 0))
            out2d[pl.ds(i, N, stride=C), :] = nn(xi_ref[...], jnp.concatenate([hi, hi, lo], 0))
        pltpu.make_async_copy(sb_ref.at[me], back_ref.at[me], local).start()
        others(lambda t: put(sb_ref.at[t], back_ref.at[me], send_b, recv_b, t))

    @pl.when(step == 3 * xl + msteps - 1)
    def _():
        await_all(rs_ref, recv_s)
        await_all(rs_ref, send_s)
        total = rs_ref[0]
        for r in range(1, space):
            total = total + rs_ref[r]
        sum_ref[...] = total
        await_all(ri_ref, recv_i)
        await_all(ri_ref, send_i)
        for c, s in x_forward(ri_ref.reshape(N * C, 2 * MY), xf_ref):
            for h in range(dp):
                spec_ref[lax.rem(h + half, dp), 1, c] = s[h * mh : (h + 1) * mh]
        mine_ref[...] = spec_ref[0]
        theirs_ref[...] = spec_ref[1]
        pltpu.make_async_copy(sb_ref.at[me], back_ref.at[me], local).wait()
        await_all(sb_ref, send_b)
        await_all(sb_ref, recv_b)


def pair_weight_kernel(mine_ref, other_ref, eo_ref, ei_ref, out_ref, *, step):
    mh = mine_ref.shape[2]
    rows = 2 * C * mh
    half = rows // 2
    for u in range(step):
        m = pl.program_id(0) * step + u
        real = imag = None
        for ref in (mine_ref, other_ref):
            flat = ref.reshape(rows, 2 * MY)
            gs = flat[pl.ds(m, C, stride=mh), :]
            vs = flat[pl.ds(half + m, C, stride=mh), :]
            g = tn(jnp.concatenate(split(gs), 0), eo_ref[...])
            i = tn(jnp.concatenate(split(vs), 0), ei_ref[...])
            gr, gi, ir, ii = g[:MY], g[MY:], i[:MY], i[MY:]
            r = gr * ir + gi * ii
            j = gi * ir - gr * ii
            real, imag = (r, j) if real is None else (real + r, imag + j)
        out_ref[u, :, : C * C] = real
        out_ref[u, :, C * C :] = imag


def restore_kernel(b_ref, sk0_ref, sk1_ref, yi_ref, zi_ref, out_ref, re_ref, im_ref):
    hi, lo = split(b_ref.reshape(MZ * C, 2 * MY)[...])
    v = nn(jnp.concatenate([hi, lo, hi], 1), yi_ref[...])
    re_ref[...] = v[:, :N]
    im_ref[...] = v[:, N:]
    for first in range(0, C, 16):
        turned = []
        for q in range(first, first + 16, 4):
            pieces = []
            for i in range(q, q + 4):
                at = pl.ds(i, MZ, stride=C)
                pieces += [re_ref[at, :], im_ref[at, :]]
            turned.append(jnp.concatenate(pieces, 0).T)
        hi, lo = split(jnp.concatenate(turned, 0))
        r = nn(jnp.concatenate([hi, lo, hi], 1), zi_ref[...])
        sk_ref = sk1_ref if first else sk0_ref
        for k in range(16):
            rows = slice(k // 4 * N, (k // 4 + 1) * N)
            cols = slice(k % 4 * N, (k % 4 + 1) * N)
            out_ref[0, first + k, 0] = sk_ref[0, k, 0] + r[rows, cols]


def fused_body(space, dp, inputs, preact, cotangent, spectral_weight, skip_weight):
    t = {k: jnp.asarray(v) for k, v in make_tables().items()}
    xl = inputs.shape[2]
    kl = spectral_weight.shape[1]
    mh = MX // dp
    field = jax.ShapeDtypeStruct(inputs.shape, F32)
    wstep = 4
    last = MX // wstep - 1
    nbytes = inputs.size * 4

    late = 2 * xl + MX // wstep

    def twice(s):
        return (0, 0, jnp.where(s < late, jnp.clip(s - xl, 0, xl - 1), s - late), 0, 0)

    def plane(first):
        return pl.BlockSpec((1, C, 1, N, N), lambda s: (0, 0, jnp.clip(s - first, 0, xl - 1), 0, 0))

    arrive = (space, xl, C, 2 * MY)
    send = (xl, space, C, 2 * MY)
    half_shape = (2, C, mh, 2 * MY)
    spec_shape = (dp,) + half_shape
    dma = pltpu.SemaphoreType.DMA
    skip_term, mine, send_half, summed, back = pl.pallas_call(
        functools.partial(fused_kernel, space=space, dp=dp, xl=xl, wstep=wstep),
        grid=(late + xl,),
        in_specs=[
            plane(0),
            plane(0),
            pl.BlockSpec((1, C, 1, N, N), twice),
            pl.BlockSpec(
                (wstep, kl, 2 * C * C), lambda s: (jnp.clip(s - 2 * xl, 0, last), 0, 0)
            ),
            whole(skip_weight.shape),
            whole(t["zf"].shape),
            whole(t["yf"].shape),
            whole(t["xf"].shape),
            whole(t["xi"].shape),
            whole(t["eo"].shape),
        ],
        out_specs=[
            plane(late),
            whole(half_shape),
            whole(half_shape),
            whole((C, 128)),
            pl.BlockSpec(memory_space=pl.ANY),
        ],
        out_shape=[
            field,
            jax.ShapeDtypeStruct(half_shape, F32),
            jax.ShapeDtypeStruct(half_shape, F32),
            jax.ShapeDtypeStruct((C, 128), F32),
            jax.ShapeDtypeStruct(arrive, F32),
        ],
        scratch_shapes=[
            pltpu.VMEM((xl, C, N, N), F32),
            pltpu.VMEM((8 * C, 24 * C), BF),
            pltpu.VMEM((8 * C, 8 * C), F32),
            pltpu.VMEM(send, F32),
            pltpu.VMEM(send, F32),
            pltpu.VMEM(arrive, F32),
            pltpu.VMEM(spec_shape, F32),
            pltpu.VMEM(arrive, F32),
            pltpu.VMEM(arrive, F32),
            pltpu.VMEM((C * MX, 2 * MY), F32),
            pltpu.VMEM((C, 128), F32),
            pltpu.VMEM((space, C, 128), F32),
        ]
        + [dma] * 9,
        compiler_params=pltpu.CompilerParams(
            vmem_limit_bytes=FUSED_LIMIT, collective_id=0, has_side_effects=True
        ),
        cost_estimate=cost(nbytes * 1500, nbytes * 5),
        name="fused_forward",
    )(
        preact, cotangent, inputs, spectral_weight, skip_weight,
        t["zf"], t["yf"], t["xf"], t["xi"], t["eo"],
    )
    pairs = [(0, 1), (1, 0)]
    theirs = lax.ppermute(send_half, "dp", pairs)
    skip_grad = NORM * (summed + lax.ppermute(summed, "dp", pairs))[:, :C]
    input_grad = pl.pallas_call(
        restore_kernel,
        grid=(xl,),
        in_specs=[
            pl.BlockSpec((MZ, 1, C, 2 * MY), lambda x: (0, x, 0, 0)),
            pl.BlockSpec((1, C // 2, 1, N, N), lambda x: (0, 0, x, 0, 0)),
            pl.BlockSpec((1, C // 2, 1, N, N), lambda x: (0, 1, x, 0, 0)),
            whole(t["yi"].shape),
            whole(t["zi4"].shape),
        ],
        out_specs=pl.BlockSpec((1, C, 1, N, N), lambda x: (0, 0, x, 0, 0)),
        out_shape=field,
        scratch_shapes=[pltpu.VMEM((MZ * C, N), F32)] * 2,
        compiler_params=params(),
        cost_estimate=cost(nbytes * 300, nbytes * 2),
        name="inverse",
    )(back, skip_term, skip_term, t["yi"], t["zi4"])
    step = 2
    weight_grad = pl.pallas_call(
        functools.partial(pair_weight_kernel, step=step),
        grid=(mh // step,),
        in_specs=[
            whole(half_shape),
            whole(half_shape),
            whole(t["eo"].shape),
            whole(t["ei"].shape),
        ],
        out_specs=pl.BlockSpec((step, kl, 2 * C * C), lambda m: (m, 0, 0)),
        out_shape=jax.ShapeDtypeStruct((mh, kl, 2 * C * C), F32),
        compiler_params=params(),
        cost_estimate=cost(1e9, mh * kl * 2 * C * C * 4),
        name="weight_grad",
    )(mine, theirs, t["eo"], t["ei"])
    return input_grad, weight_grad, skip_grad


def solution(mesh):
    in_specs = (
        P("dp", None, "space", None, None),
        P("dp", None, "space", None, None),
        P("dp", None, "space", None, None),
        P(None, "space", None),
        P(),
    )
    out_specs = (P("dp", None, "space", None, None), P("dp", "space", None), P())
    space, dp = mesh.shape["space"], mesh.shape["dp"]
    form = fused_body if space == MZ and dp == 2 else body
    local = functools.partial(form, space, dp)
    return jax.shard_map(local, mesh=mesh, in_specs=in_specs, out_specs=out_specs, check_vma=False)
```
